128 devices in a mesh: dp: 16 (over y, z), mp: 8 (over x, core).
Axes of the slice: x: 4, y: 4, z: 4, core: 2. Of those that a mesh axis runs over, the one named last changes fastest.
Arguments:
- grad_kv: bfloat16 [16, 2, 8192, 1024], P('dp', None, None, 'mp'), may hold values from -9 to 9
- error_kv: bfloat16 [16, 2, 8192, 1024], P('dp', None, None, 'mp'), may hold values from -3 to 3
- grad_out: bfloat16 [16, 4096, 4096], P('dp', None, 'mp'), may hold values from -9 to 9
- error_out: bfloat16 [16, 4096, 4096], P('dp', None, 'mp'), may hold values from -3 to 3
- basis_kv: float32 [2, 1024, 32], P(None, 'mp'), may hold values from -6 to 6
- basis_out: float32 [4096, 32], P('mp'), may hold values from -6 to 6
Outputs:
- left_kv: float32 [2, 8192, 32], replicated
- left_out: float32 [4096, 32], replicated
- right_kv: float32 [2, 1024, 32], P(None, 'mp')
- right_out: float32 [4096, 32], P('mp')
- new_error_kv: bfloat16 [16, 2, 8192, 1024], P('dp', None, None, 'mp')
- new_error_out: bfloat16 [16, 4096, 4096], P('dp', None, 'mp')
The draws below stay inside these ranges and needn't reach their ends.
All inputs are finite; a program needn't handle non-finite values.
Results may differ from the reference program's by a relative error of at most 0.001.
Values sent between devices are 32-bit elements; how exact they have to be, the bound alone decides.
No kernel may reach another device: no remote copies, remote signals or barrier semaphores. Data moves between devices by JAX's collectives and lax.ppermute only.
A program may use at most 128 MiB of HBM per device.

```python
import jax
import jax.numpy as jnp
from jax import lax

D = 8192
KV = 1024
OROWS = 4096
OCOLS = 4096
RANK = 32
REPLICAS = 16


def shared_plus_own(key, shape):
    base_key, own_key = jax.random.split(key)
    base = jnp.clip(jax.random.normal(base_key, (1,) + shape[1:], jnp.float32), -6.0, 6.0)
    own = jnp.clip(jax.random.normal(own_key, shape, jnp.float32), -6.0, 6.0)
    return (base + 0.5 * own).astype(jnp.bfloat16)


def draw_grad_kv(key, part):
    key = jax.random.fold_in(key, 11)
    return shared_plus_own(key, (REPLICAS, 2, D, KV))


def draw_grad_out(key, part):
    key = jax.random.fold_in(key, 23)
    return shared_plus_own(key, (REPLICAS, OROWS, OCOLS))


def block_levels(key, extent, pieces, least, top_value):
    def one(axis_at, blocks):
        steps = jax.random.uniform(jax.random.fold_in(jax.random.fold_in(key, 6), axis_at), (blocks,), jnp.float32, least / len(pieces), top_value / len(pieces))
        return jnp.repeat(jnp.exp(steps), extent[axis_at] // blocks).reshape((-1,) + (1,) * (len(extent) - axis_at - 1))

    level = one(*pieces[0])
    for cut in pieces[1:]:
        level = level * one(*cut)
    return level


def noise(stream_key, shape, width, bound, cuts=(), kind=jnp.bfloat16):
    loudness = block_levels(stream_key, shape, cuts, -0.22, 0.18) if cuts else 1.0
    drawn = jax.random.normal(stream_key, shape, jnp.float32) * width * loudness
    return jnp.minimum(jnp.maximum(drawn, -bound), bound).astype(kind)


def setup_inputs(seed: int = 0) -> dict:
    keys = jax.random.split(jax.random.key(seed), 7)
    return {
        "grad_kv": draw_grad_kv(jax.random.fold_in(keys[6], 71), 0),
        "error_kv": noise(keys[1], (REPLICAS, 2, D, KV), 0.5, 3.0, ((0, 16), (3, 8))),
        "grad_out": draw_grad_out(jax.random.fold_in(keys[6], 71), 0),
        "error_out": noise(keys[3], (REPLICAS, OROWS, OCOLS), 0.5, 3.0, ((0, 16), (2, 8))),
        "basis_kv": noise(keys[4], (2, KV, RANK), 1.0, 6.0, ((1, 8),), jnp.float32),
        "basis_out": noise(keys[5], (OCOLS, RANK), 1.0, 6.0, ((0, 8),), jnp.float32),
    }


HIGH = lax.Precision.HIGHEST

def orthonormal(lead):
    gram = jnp.einsum('...dr,...ds->...rs', lead, lead, precision=HIGH)
    low = jnp.linalg.cholesky(gram)
    return lax.linalg.triangular_solve(low, lead, left_side=False, lower=True, transpose_a=True)

def reference(grad_kv, error_kv, grad_out, error_out, basis_kv, basis_out):

    def merge_pair(items):
        gk, ek, go, eo = items
        return (gk.astype(jnp.float32) + ek.astype(jnp.float32), go.astype(jnp.float32) + eo.astype(jnp.float32))

    def lead_step(carry, items):
        mk, mo = merge_pair(items)
        return ((carry[0] + jnp.einsum('adc,acr->adr', mk, basis_kv, precision=HIGH), carry[1] + jnp.dot(mo, basis_out, precision=HIGH)), None)
    start = (jnp.zeros((2, D, RANK), jnp.float32), jnp.zeros((OROWS, RANK), jnp.float32))
    items = (grad_kv, error_kv, grad_out, error_out)
    (lead_kv, lead_out), _ = lax.scan(lead_step, start, items)
    ortho_kv = orthonormal(lead_kv)
    ortho_out = orthonormal(lead_out)

    def right_step(carry, items):
        mk, mo = merge_pair(items)
        return ((carry[0] + jnp.einsum('adc,adr->acr', mk, ortho_kv, precision=HIGH), carry[1] + jnp.dot(mo.T, ortho_out, precision=HIGH)), None)
    start = (jnp.zeros((2, KV, RANK), jnp.float32), jnp.zeros((OCOLS, RANK), jnp.float32))
    (sum_kv, sum_out), _ = lax.scan(right_step, start, items)
    right_kv = sum_kv / REPLICAS
    right_out = sum_out / REPLICAS

    def error_one(items):
        mk, mo = merge_pair(items)
        ek = mk - jnp.einsum('adr,acr->adc', ortho_kv, right_kv, precision=HIGH)
        eo = mo - jnp.dot(ortho_out, right_out.T, precision=HIGH)
        return (ek.astype(jnp.bfloat16), eo.astype(jnp.bfloat16))
    new_kv, new_out = lax.map(error_one, items)
    left_kv = jnp.sqrt(jnp.float32(D)) * ortho_kv
    left_out = jnp.sqrt(jnp.float32(OROWS)) * ortho_out
    return (left_kv, left_out, right_kv, right_out, new_kv, new_out)
```

```python
import functools

import jax
import jax.numpy as jnp
from jax import lax
from jax.experimental import pallas as pl
from jax.experimental.pallas import tpu as pltpu
from jax.sharding import PartitionSpec as P

F32, BF16 = jnp.float32, jnp.bfloat16
ROWS, COLS = 8192, 128
OROWS, OCOLS = 4096, 512
RANK = 32
REPLICAS = 16
CH = ROWS // 8
OCH = OROWS // 8
HALF = OCH // 2
WIDE = CH + HALF
MIB = 1 << 20


def exchange(axis, turn):
    pairs = []
    for i in range(128):
        q, core = [(i // 2) % 4, i // 32, (i // 8) % 4], i % 2
        q[axis] ^= 1 if turn == core else 3
        pairs.append((i, ((q[1] * 4 + q[2]) * 4 + q[0]) * 2 + core))
    return pairs


CORES = [(i, i ^ 1) for i in range(128)]


def send(x, pairs):
    return lax.ppermute(x, ("dp", "mp"), pairs)


def my_chunk(dh, du, dv):
    dp, mp = lax.axis_index("dp"), lax.axis_index("mp")
    x, y = lax.div(mp, 2), lax.div(dp, 4)
    half = jnp.bitwise_xor(lax.rem(mp, 2), dh)

    def own(q):
        high, low = lax.div(q, 2), lax.rem(q, 2)
        return jnp.bitwise_xor(high, low * (1 - half))

    u = jnp.bitwise_xor(own(x), du)
    v = jnp.bitwise_xor(own(y), dv)
    return half * 4 + u * 2 + v


def dot_nt(a, b):
    return lax.dot_general(a, b, (((1,), (1,)), ((), ())), preferred_element_type=F32)


def dot(a, b):
    return jnp.dot(a, b, preferred_element_type=F32)


def split2(a):
    high = a.astype(BF16)
    return high, (a - high.astype(F32)).astype(BF16)


def split3(a):
    high = a.astype(BF16)
    rest = a - high.astype(F32)
    mid = rest.astype(BF16)
    return high, mid, (rest - mid.astype(F32)).astype(BF16)


def loads(refs, bufs, sems, slot, chunk):
    rows = pl.ds(pl.multiple_of(chunk * CH, CH), CH)
    orows = pl.ds(pl.multiple_of(chunk * OCH, OCH), OCH)
    gkv, ekv, gout, eout = refs
    bgkv, bekv, bgout, beout = bufs
    return [
        pltpu.make_async_copy(gkv.at[0, :, rows, :], bgkv.at[slot], sems.at[slot, 0]),
        pltpu.make_async_copy(ekv.at[0, :, rows, :], bekv.at[slot], sems.at[slot, 1]),
        pltpu.make_async_copy(gout.at[0, orows, :], bgout.at[slot], sems.at[slot, 2]),
        pltpu.make_async_copy(eout.at[0, orows, :], beout.at[slot], sems.at[slot, 3]),
    ]


def buffers(n):
    return [
        pltpu.VMEM((n, 2, CH, COLS), BF16),
        pltpu.VMEM((n, 2, CH, COLS), BF16),
        pltpu.VMEM((n, OCH, OCOLS), BF16),
        pltpu.VMEM((n, OCH, OCOLS), BF16),
        pltpu.SemaphoreType.DMA((n, 4)),
    ]


ANY = pl.BlockSpec(memory_space=pl.ANY)
VM = pl.BlockSpec(memory_space=pltpu.VMEM)


def part_kernel(dh, gkv, ekv, gout, eout, bkv, bout, out, bgkv, bekv, bgout, beout, sems):
    copies = [
        loads((gkv, ekv, gout, eout), (bgkv, bekv, bgout, beout), sems, j, my_chunk(dh, j // 2, j % 2))
        for j in range(4)
    ]
    for chunk in copies:
        for copy in chunk:
            copy.start()
    kv = [jnp.concatenate(split3(bkv[a]), axis=0) for a in range(2)]
    kv = [jnp.concatenate([b, b], axis=1) for b in kv]
    ob = jnp.concatenate(split3(bout[...]), axis=0)

    def fold(r):
        return r[:RANK] + (r[RANK : 2 * RANK] + r[2 * RANK :])

    for j in range(4):
        for copy in copies[j]:
            copy.wait()
        for a in range(2):
            both = jnp.concatenate([bgkv[j, a], bekv[j, a]], axis=1)
            out[j, a, :, :CH] = fold(dot_nt(kv[a], both))
        o = fold(dot_nt(ob, bgout[j]) + dot_nt(ob, beout[j]))
        out[j, 0, :, CH:] = o[:, :HALF]
        out[j, 1, :, CH:] = o[:, HALF:]


def part(dh, args):
    return pl.pallas_call(
        functools.partial(part_kernel, dh),
        out_shape=jax.ShapeDtypeStruct((4, 2, RANK, WIDE), F32),
        in_specs=[ANY] * 4 + [VM] * 2,
        out_specs=VM,
        scratch_shapes=buffers(4),
        compiler_params=pltpu.CompilerParams(vmem_limit_bytes=20 * MIB),
        cost_estimate=pl.CostEstimate(flops=800_000_000, bytes_accessed=9 * MIB, transcendentals=0),
        name="part",
    )(*args)


def piece(refs, du, dv):
    a_own, a_got, b_own, b_got = refs
    return (a_got if du else a_own)[dv], (b_got if dv else b_own)[du]


def right_kernel(dh, first, *refs):
    gkv, ekv, gout, eout = refs[:4]
    lead = refs[4:8]
    before = () if first else refs[8:10]
    right, gram, bgkv, bekv, bgout, beout, sems = refs[8 if first else 10 :]
    copies = [
        loads((gkv, ekv, gout, eout), (bgkv, bekv, bgout, beout), sems, j, my_chunk(dh, j // 2, j % 2))
        for j in range(4)
    ]
    for chunk in copies:
        for copy in chunk:
            copy.start()

    def fold(r):
        return r[:RANK] + r[RANK:]

    def square(parts):
        g = dot_nt(jnp.concatenate(parts, axis=0), jnp.concatenate(parts, axis=0))

        def at(i, j):
            return g[i * RANK : (i + 1) * RANK, j * RANK : (j + 1) * RANK]

        return at(0, 0) + ((at(0, 1) + at(1, 0)) + ((at(0, 2) + at(2, 0)) + at(1, 1)))

    grams = []
    sums = None
    for j in range(4):
        a, b = piece(lead, j // 2, j % 2)
        pa, pb = split3(a), split3(b)
        kva, kvb = [p[:, :CH] for p in pa], [p[:, :CH] for p in pb]
        oa, ob = [p[:, CH:] for p in pa], [p[:, CH:] for p in pb]
        o = [jnp.concatenate([p, q], axis=1) for p, q in zip(oa, ob)]
        grams.append([square(kva), square(kvb), square(o)])
        for copy in copies[j]:
            copy.wait()
        terms = []
        for k, parts in enumerate((kva, kvb)):
            both = jnp.concatenate([bgkv[j, k], bekv[j, k]], axis=1)
            r = fold(dot(jnp.concatenate(parts[:2], axis=0), both))
            terms.append(r[:, :COLS] + r[:, COLS:])
        two = jnp.concatenate(o[:2], axis=0)
        terms.append(fold(dot(two, bgout[j]) + dot(two, beout[j])))
        sums = terms if sums is None else [s + t for s, t in zip(sums, terms)]
    for k in range(3):
        gram_k = (grams[0][k] + grams[1][k]) + (grams[2][k] + grams[3][k])
        gram[k] = gram_k if first else gram_k + before[1][k]
    sums = jnp.concatenate(sums, axis=1)
    right[...] = sums if first else sums + before[0][...]


def right_part(dh, args, lead, before=()):
    return pl.pallas_call(
        functools.partial(right_kernel, dh, not before),
        out_shape=(
            jax.ShapeDtypeStruct((RANK, 2 * COLS + OCOLS), F32),
            jax.ShapeDtypeStruct((3, RANK, RANK), F32),
        ),
        in_specs=[ANY] * 4 + [VM] * (4 + len(before)),
        out_specs=(VM, VM),
        scratch_shapes=buffers(4),
        compiler_params=pltpu.CompilerParams(vmem_limit_bytes=20 * MIB),
        cost_estimate=pl.CostEstimate(flops=800_000_000, bytes_accessed=9 * MIB, transcendentals=0),
        name="right",
    )(*args, *lead, *before)


def factor_kernel(gram, out):
    row = lax.broadcasted_iota(jnp.int32, (RANK, 2 * RANK), 0)
    col = lax.broadcasted_iota(jnp.int32, (RANK, 2 * RANK), 1)
    eye = jnp.where(col == row + RANK, 1.0, 0.0).astype(F32)
    wide = [jnp.concatenate([gram[k], jnp.zeros((RANK, RANK), F32)], axis=1) + eye for k in range(3)]
    scale = [jnp.zeros((RANK, 1), F32)] * 3
    below = lax.broadcasted_iota(jnp.int32, (RANK, 1), 0)
    for i in range(RANK):
        for k in range(3):
            pivot = wide[k][i : i + 1, :]
            d = wide[k][i : i + 1, i : i + 1]
            scale[k] = jnp.where(below == i, lax.rsqrt(d), scale[k])
            factor = jnp.where(below > i, wide[k][:, i : i + 1] / d, 0.0)
            wide[k] = wide[k] - factor * pivot
    for k in range(3):
        out[k] = wide[k][:, RANK:] * scale[k]


def factor(gram):
    return pl.pallas_call(
        factor_kernel,
        out_shape=jax.ShapeDtypeStruct((3, RANK, RANK), F32),
        in_specs=[VM],
        out_specs=VM,
        cost_estimate=pl.CostEstimate(flops=10_000_000, bytes_accessed=3 * MIB, transcendentals=0),
        name="factor",
    )(gram)


def left_kernel(*refs):
    own, other, w = refs[:4], refs[4:8], refs[8]
    left_kv, left_out, ortho = refs[9:12]
    bkv, bout, sems = refs[12:]
    weights = []
    for k in range(3):
        w1, w2, w3 = split3(w[k])
        weights.append(jnp.concatenate([w1, w1, w2, w1, w2, w3], axis=1))

    def apply(k, x):
        l1, l2, l3 = split3(x)
        return dot(weights[k], jnp.concatenate([l1, l2, l1, l3, l2, l1], axis=0))

    def packed(o):
        high = o.astype(BF16).astype(F32)
        rest = o - high
        return jnp.transpose(jnp.concatenate([high, rest, high, jnp.zeros_like(o)], axis=0)).astype(BF16)

    copies = []
    for j in range(8):
        dh, du, dv = j // 4, (j // 2) % 2, j % 2
        a, b = piece(other if dh else own, du, dv)
        out = []
        for s, x in enumerate((a, b)):
            o_kv = apply(s, x[:, :CH])
            o_out = apply(2, x[:, CH:])
            bkv[j, s] = o_kv * (ROWS**0.5)
            out.append(o_out * (OROWS**0.5))
            ortho[j, s, :CH] = packed(o_kv)
            ortho[j, s, CH:] = packed(o_out)
        bout[j, :, :HALF] = out[0]
        bout[j, :, HALF:] = out[1]
        t = my_chunk(dh, du, dv)
        cols = pl.ds(pl.multiple_of(t * CH, CH), CH)
        ocols = pl.ds(pl.multiple_of(t * OCH, OCH), OCH)
        copies.append(pltpu.make_async_copy(bkv.at[j], left_kv.at[:, :, cols], sems.at[j, 0]))
        copies.append(pltpu.make_async_copy(bout.at[j], left_out.at[:, ocols], sems.at[j, 1]))
        copies[-2].start()
        copies[-1].start()
    for copy in copies:
        copy.wait()


def left_part(own, other, w):
    return pl.pallas_call(
        left_kernel,
        out_shape=(
            jax.ShapeDtypeStruct((2, RANK, ROWS), F32),
            jax.ShapeDtypeStruct((RANK, OROWS), F32),
            jax.ShapeDtypeStruct((8, 2, WIDE, 128), BF16),
        ),
        in_specs=[VM] * 9,
        out_specs=(ANY, ANY, VM),
        scratch_shapes=[
            pltpu.VMEM((8, 2, RANK, CH), F32),
            pltpu.VMEM((8, RANK, OCH), F32),
            pltpu.SemaphoreType.DMA((8, 2)),
        ],
        compiler_params=pltpu.CompilerParams(vmem_limit_bytes=24 * MIB),
        cost_estimate=pl.CostEstimate(flops=500_000_000, bytes_accessed=10 * MIB, transcendentals=0),
        name="left",
    )(*own, *other, w)


def error_kernel(*refs):
    gkv, ekv, gout, eout, total, w, ortho = refs[:7]
    right_kv, right_out, new_kv, new_out = refs[7:11]
    bgkv, bekv, bgout, beout, sems, nkv, nout, nsems = refs[11:]
    chunks = [my_chunk(j // 4, (j // 2) % 2, j % 2) for j in range(8)]
    copies = [loads((gkv, ekv, gout, eout), (bgkv, bekv, bgout, beout), sems, j, chunks[j]) for j in range(8)]
    for chunk in copies:
        for copy in chunk:
            copy.start()
    packed = []
    for k, (at, n) in enumerate(((0, COLS), (COLS, COLS), (2 * COLS, OCOLS))):
        w1, w2, w3 = split3(w[k])
        r1, r2, r3 = split3(total[:, at : at + n] * (1.0 / REPLICAS))
        right = dot(
            jnp.concatenate([w1, w1, w2, w1, w2, w3], axis=1),
            jnp.concatenate([r1, r2, r1, r3, r2, r1], axis=0),
        )
        if k < 2:
            right_kv[k] = right
        else:
            right_out[...] = right
        high, low = split2(right)
        packed.append(jnp.concatenate([high, high, low, jnp.zeros_like(high)], axis=0))
    stores = []
    for j in range(8):
        for copy in copies[j]:
            copy.wait()
        for s in range(2):
            merged = bgkv[j, s].astype(F32) + bekv[j, s].astype(F32)
            nkv[j, s] = (merged - dot(ortho[j, s, :CH], packed[s])).astype(BF16)
            rows = slice(s * HALF, (s + 1) * HALF)
            merged = bgout[j, rows].astype(F32) + beout[j, rows].astype(F32)
            nout[j, rows] = (merged - dot(ortho[j, s, CH:], packed[2])).astype(BF16)
        rows = pl.ds(pl.multiple_of(chunks[j] * CH, CH), CH)
        orows = pl.ds(pl.multiple_of(chunks[j] * OCH, OCH), OCH)
        stores.append(pltpu.make_async_copy(nkv.at[j], new_kv.at[0, :, rows, :], nsems.at[j, 0]))
        stores.append(pltpu.make_async_copy(nout.at[j], new_out.at[0, orows, :], nsems.at[j, 1]))
        stores[-2].start()
        stores[-1].start()
    for copy in stores:
        copy.wait()


def errors(args, total, w, ortho):
    return pl.pallas_call(
        error_kernel,
        out_shape=(
            jax.ShapeDtypeStruct((2, RANK, COLS), F32),
            jax.ShapeDtypeStruct((RANK, OCOLS), F32),
            jax.ShapeDtypeStruct((1, 2, ROWS, COLS), BF16),
            jax.ShapeDtypeStruct((1, OROWS, OCOLS), BF16),
        ),
        in_specs=[ANY] * 4 + [VM] * 3,
        out_specs=(VM, VM, ANY, ANY),
        scratch_shapes=buffers(8)
        + [
            pltpu.VMEM((8, 2, CH, COLS), BF16),
            pltpu.VMEM((8, OCH, OCOLS), BF16),
            pltpu.SemaphoreType.DMA((8, 2)),
        ],
        compiler_params=pltpu.CompilerParams(vmem_limit_bytes=40 * MIB),
        cost_estimate=pl.CostEstimate(flops=800_000_000, bytes_accessed=29 * MIB, transcendentals=0),
        name="errors",
    )(*args, total, w, ortho)


X, Y, Z = 0, 1, 2


def on_device(grad_kv, error_kv, grad_out, error_out, basis_kv, basis_out):
    grads = (grad_kv, error_kv, grad_out, error_out)
    args = (*grads, jnp.swapaxes(basis_kv, 1, 2), basis_out.T)
    got = send(part(1, args), CORES)
    kept = part(0, args) + got
    a, b = [kept[:, s].reshape(2, 2, RANK, WIDE) for s in range(2)]

    a = a[0] + send(a[1], exchange(X, 0))
    b = b[:, 0] + send(b[:, 1], exchange(Y, 0))
    a = a[0] + send(a[1], exchange(Y, 0))
    b = b[0] + send(b[1], exchange(X, 0))
    for axis_a, axis_b in (((Z, 0), (Y, 1)), ((X, 1), (Z, 0)), ((Z, 1), (X, 1)), ((Y, 1), (Z, 1))):
        a, b = a + send(a, exchange(*axis_a)), b + send(b, exchange(*axis_b))
    a_own = jnp.stack([a, send(a, exchange(Y, 0))])
    b_own = jnp.stack([b, send(b, exchange(X, 0))])
    a_got = send(a_own, exchange(X, 0))
    b_got = send(b_own, exchange(Y, 0))
    own = (a_own, a_got, b_own, b_got)
    other = [send(p, CORES) for p in own]

    total, gram = right_part(1, grads, other, right_part(0, grads, own))
    w = factor(gram)
    left_kv, left_out, ortho = left_part(own, other, w)
    for axis, turn in ((Y, 0), (Z, 0), (Y, 1), (Z, 1)):
        total = total + send(total, exchange(axis, turn))
    right_kv, right_out, new_kv, new_out = errors(grads, total, w, ortho)
    return (
        jnp.swapaxes(left_kv, 1, 2),
        left_out.T,
        jnp.swapaxes(right_kv, 1, 2),
        right_out.T,
        new_kv,
        new_out,
    )


def solution(mesh):
    placed = (
        P("dp", None, None, "mp"),
        P("dp", None, None, "mp"),
        P("dp", None, "mp"),
        P("dp", None, "mp"),
        P(None, "mp", None),
        P("mp", None),
    )
    return jax.shard_map(
        on_device,
        mesh=mesh,
        in_specs=placed,
        out_specs=(
            P(),
            P(),
            P(None, "mp", None),
            P("mp", None),
            P("dp", None, None, "mp"),
            P("dp", None, "mp"),
        ),
        check_vma=False,
    )
```

```python
import functools

import jax
import jax.numpy as jnp
from jax import lax
from jax.experimental import pallas as pl
from jax.experimental.pallas import tpu as pltpu
from jax.sharding import PartitionSpec as P

F32, BF16 = jnp.float32, jnp.bfloat16
ROWS, COLS = 8192, 128
OROWS, OCOLS = 4096, 512
RANK = 32
REPLICAS = 16
CH = ROWS // 8
OCH = OROWS // 8
HALF = OCH // 2
WIDE = CH + HALF
MIB = 1 << 20


def exchange(axis, turn):
    pairs = []
    for i in range(128):
        q, core = [(i // 2) % 4, i // 32, (i // 8) % 4], i % 2
        q[axis] ^= 1 if turn == core else 3
        pairs.append((i, ((q[1] * 4 + q[2]) * 4 + q[0]) * 2 + core))
    return pairs


CORES = [(i, i ^ 1) for i in range(128)]


def send(x, pairs):
    return lax.ppermute(x, ("dp", "mp"), pairs)


def my_chunk(dh, du, dv):
    dp, mp = lax.axis_index("dp"), lax.axis_index("mp")
    x, y = lax.div(mp, 2), lax.div(dp, 4)
    half = jnp.bitwise_xor(lax.rem(mp, 2), dh)

    def own(q):
        high, low = lax.div(q, 2), lax.rem(q, 2)
        return jnp.bitwise_xor(high, low * (1 - half))

    u = jnp.bitwise_xor(own(x), du)
    v = jnp.bitwise_xor(own(y), dv)
    return half * 4 + u * 2 + v


def dot_nt(a, b):
    return lax.dot_general(a, b, (((1,), (1,)), ((), ())), preferred_element_type=F32)


def dot(a, b):
    return jnp.dot(a, b, preferred_element_type=F32)


def split2(a):
    high = a.astype(BF16)
    return high, (a - high.astype(F32)).astype(BF16)


def split3(a):
    high = a.astype(BF16)
    rest = a - high.astype(F32)
    mid = rest.astype(BF16)
    return high, mid, (rest - mid.astype(F32)).astype(BF16)


def loads(refs, bufs, sems, slot, chunk):
    rows = pl.ds(pl.multiple_of(chunk * CH, CH), CH)
    orows = pl.ds(pl.multiple_of(chunk * OCH, OCH), OCH)
    gkv, ekv, gout, eout = refs
    bgkv, bekv, bgout, beout = bufs
    return [
        pltpu.make_async_copy(gkv.at[0, :, rows, :], bgkv.at[slot], sems.at[slot, 0]),
        pltpu.make_async_copy(ekv.at[0, :, rows, :], bekv.at[slot], sems.at[slot, 1]),
        pltpu.make_async_copy(gout.at[0, orows, :], bgout.at[slot], sems.at[slot, 2]),
        pltpu.make_async_copy(eout.at[0, orows, :], beout.at[slot], sems.at[slot, 3]),
    ]


ANY = pl.BlockSpec(memory_space=pl.ANY)
HBM = pl.BlockSpec(memory_space=pltpu.HBM)
VM = pl.BlockSpec(memory_space=pltpu.VMEM)


def cost(us):
    return pl.CostEstimate(flops=0, bytes_accessed=int(us * 3_000_000), transcendentals=0)


def part_kernel(dh, gkv, ekv, gout, eout, bkv_hbm, bout_hbm, out, bgkv, bekv, bgout, beout, bkv, bout, bsems, sems):
    basis = [
        pltpu.make_async_copy(bkv_hbm, bkv, bsems.at[0]),
        pltpu.make_async_copy(bout_hbm, bout, bsems.at[1]),
    ]
    copies = [
        loads((gkv, ekv, gout, eout), (bgkv, bekv, bgout, beout), sems, j, my_chunk(dh, j // 2, j % 2))
        for j in range(4)
    ]
    for copy in basis:
        copy.start()
    for chunk in copies:
        for copy in chunk:
            copy.start()
    for copy in basis:
        copy.wait()
    kv = [jnp.concatenate(split3(bkv[a]), axis=0) for a in range(2)]
    kv = [jnp.concatenate([b, b], axis=1) for b in kv]
    ob = jnp.concatenate(split3(bout[...]), axis=0)

    def fold(r):
        return r[:RANK] + (r[RANK : 2 * RANK] + r[2 * RANK :])

    for j in range(4):
        for copy in copies[j]:
            copy.wait()
        for a in range(2):
            both = jnp.concatenate([bgkv[j, a], bekv[j, a]], axis=1)
            out[a, j, :, :CH] = fold(dot_nt(kv[a], both))
        o = fold(dot_nt(ob, bgout[j]) + dot_nt(ob, beout[j]))
        out[0, j, :, CH:] = o[:, :HALF]
        out[1, j, :, CH:] = o[:, HALF:]


def part(dh, args):
    kv = jax.ShapeDtypeStruct((4, 2, CH, COLS), BF16)
    out = jax.ShapeDtypeStruct((4, OCH, OCOLS), BF16)
    result = pl.pallas_call(
        functools.partial(part_kernel, dh),
        out_shape=(jax.ShapeDtypeStruct((2, 4, RANK, WIDE), F32), kv, kv, out, out),
        in_specs=[HBM] * 6,
        out_specs=(VM,) * 5,
        scratch_shapes=[
            pltpu.VMEM((2, RANK, COLS), F32),
            pltpu.VMEM((RANK, OCOLS), F32),
            pltpu.SemaphoreType.DMA((2,)),
            pltpu.SemaphoreType.DMA((4, 4)),
        ],
        compiler_params=pltpu.CompilerParams(vmem_limit_bytes=20 * MIB),
        cost_estimate=cost(4),
        name="part",
    )(*args)
    return result[0], result[1:]


def right_kernel(got, n_before, *refs):
    bgkv, bekv, bgout, beout, lead_a, lead_b = refs[:6]
    before = refs[6 : 6 + n_before]
    right, gram = refs[6 + n_before :]

    def fold(r):
        return r[:RANK] + r[RANK:]

    def square(parts):
        g = dot_nt(jnp.concatenate(parts, axis=0), jnp.concatenate(parts, axis=0))

        def at(i, j):
            return g[i * RANK : (i + 1) * RANK, j * RANK : (j + 1) * RANK]

        return at(0, 0) + ((at(0, 1) + at(1, 0)) + ((at(0, 2) + at(2, 0)) + at(1, 1)))

    sums = [0.0, 0.0, 0.0]
    grams = [[], [], []]
    for j in range(2):
        for k, x in enumerate((lead_a, lead_b)):
            chunk = (got * 2 + j) if k == 0 else (j * 2 + got)
            parts = split3(x[j])
            kv, o = [p[:, :CH] for p in parts], [p[:, CH:] for p in parts]
            grams[k].append(square(kv))
            grams[2].append(square(o))
            both = jnp.concatenate([bgkv[chunk, k], bekv[chunk, k]], axis=1)
            r = fold(dot(jnp.concatenate(kv[:2], axis=0), both))
            sums[k] += r[:, :COLS] + r[:, COLS:]
            two = jnp.concatenate(o[:2], axis=0)
            rows = slice(k * HALF, (k + 1) * HALF)
            sums[2] += fold(dot(two, bgout[chunk, rows]) + dot(two, beout[chunk, rows]))
    gram[0] = grams[0][0] + grams[0][1]
    gram[1] = grams[1][0] + grams[1][1]
    gram[2] = (grams[2][0] + grams[2][2]) + (grams[2][1] + grams[2][3])
    sums = jnp.concatenate(sums, axis=1)
    for other in before:
        sums += other[...]
    right[...] = sums


def right_part(got, bufs, lead, before=()):
    return pl.pallas_call(
        functools.partial(right_kernel, got, len(before)),
        out_shape=(
            jax.ShapeDtypeStruct((RANK, 2 * COLS + OCOLS), F32),
            jax.ShapeDtypeStruct((3, RANK, RANK), F32),
        ),
        in_specs=[VM] * (6 + len(before)),
        out_specs=(VM, VM),
        compiler_params=pltpu.CompilerParams(vmem_limit_bytes=20 * MIB),
        cost_estimate=cost(2),
        name="right",
    )(*bufs, *lead, *before)


def factor_kernel(g0, g1, g2, g3, out):
    row = lax.broadcasted_iota(jnp.int32, (RANK, 2 * RANK), 0)
    col = lax.broadcasted_iota(jnp.int32, (RANK, 2 * RANK), 1)
    eye = jnp.where(col == row + RANK, 1.0, 0.0).astype(F32)
    gram = [(g0[k] + g1[k]) + (g2[k] + g3[k]) for k in range(3)]
    wide = [jnp.concatenate([gram[k], jnp.zeros((RANK, RANK), F32)], axis=1) + eye for k in range(3)]
    scale = [jnp.zeros((RANK, 1), F32)] * 3
    below = lax.broadcasted_iota(jnp.int32, (RANK, 1), 0)
    for i in range(RANK):
        for k in range(3):
            pivot = wide[k][i : i + 1, :]
            d = wide[k][i : i + 1, i : i + 1]
            scale[k] = jnp.where(below == i, lax.rsqrt(d), scale[k])
            factor = jnp.where(below > i, wide[k][:, i : i + 1] / d, 0.0)
            wide[k] = wide[k] - factor * pivot
    for k in range(3):
        out[k] = wide[k][:, RANK:] * scale[k]


def factor(grams):
    return pl.pallas_call(
        factor_kernel,
        out_shape=jax.ShapeDtypeStruct((3, RANK, RANK), F32),
        in_specs=[VM] * 4,
        out_specs=VM,
        cost_estimate=cost(4),
        name="factor",
    )(*grams)


def left_kernel(dh, *refs):
    a_own, a_got, b_own, b_got, w = refs[:5]
    left_kv, left_out, ortho, bkv, bout, sems = refs[-6:]
    weights = []
    for k in range(3):
        w1, w2, w3 = split3(w[k])
        weights.append(jnp.concatenate([w1, w1, w2, w1, w2, w3], axis=1))

    def apply(k, x):
        l1, l2, l3 = split3(x)
        return dot(weights[k], jnp.concatenate([l1, l2, l1, l3, l2, l1], axis=0))

    def packed(o):
        high = o.astype(BF16).astype(F32)
        rest = o - high
        return jnp.transpose(jnp.concatenate([high, rest, high, jnp.zeros_like(o)], axis=0)).astype(BF16)

    copies = []
    for j in range(4):
        du, dv = j // 2, j % 2
        out = []
        for s, x in enumerate(((a_got if du else a_own)[dv], (b_got if dv else b_own)[du])):
            o_kv = apply(s, x[:, :CH])
            o_out = apply(2, x[:, CH:])
            bkv[j, s] = o_kv * (ROWS**0.5)
            out.append(o_out * (OROWS**0.5))
            ortho[j, s, :CH] = packed(o_kv)
            ortho[j, s, CH:] = packed(o_out)
        bout[j, :, :HALF] = out[0]
        bout[j, :, HALF:] = out[1]
        t = my_chunk(dh, du, dv)
        cols = pl.ds(pl.multiple_of(t * CH, CH), CH)
        ocols = pl.ds(pl.multiple_of(t * OCH, OCH), OCH)
        copies.append(pltpu.make_async_copy(bkv.at[j], left_kv.at[:, :, cols], sems.at[j, 0]))
        copies.append(pltpu.make_async_copy(bout.at[j], left_out.at[:, ocols], sems.at[j, 1]))
        copies[-2].start()
        copies[-1].start()
    for copy in copies:
        copy.wait()


def left_part(dh, lead, w, before=()):
    return pl.pallas_call(
        functools.partial(left_kernel, dh),
        out_shape=(
            jax.ShapeDtypeStruct((2, RANK, ROWS), F32),
            jax.ShapeDtypeStruct((RANK, OROWS), F32),
            jax.ShapeDtypeStruct((4, 2, WIDE, 128), BF16),
        ),
        in_specs=[VM] * 5 + [HBM] * len(before),
        out_specs=(HBM, HBM, VM),
        scratch_shapes=[
            pltpu.VMEM((4, 2, RANK, CH), F32),
            pltpu.VMEM((4, RANK, OCH), F32),
            pltpu.SemaphoreType.DMA((4, 2)),
        ],
        input_output_aliases={5: 0, 6: 1} if before else {},
        compiler_params=pltpu.CompilerParams(vmem_limit_bytes=16 * MIB),
        cost_estimate=cost(2),
        name="left",
    )(*lead, w, *before)


def error_kernel(*refs):
    halves = (refs[:4], refs[4:8])
    total, w, ortho = refs[8], refs[9], refs[10:12]
    right_kv, right_out, new_kv, new_out, nkv, nout, nsems = refs[12:]
    packed = []
    for k, (at, n) in enumerate(((0, COLS), (COLS, COLS), (2 * COLS, OCOLS))):
        w1, w2, w3 = split3(w[k])
        r1, r2, r3 = split3(total[:, at : at + n] * (1.0 / REPLICAS))
        right = dot(
            jnp.concatenate([w1, w1, w2, w1, w2, w3], axis=1),
            jnp.concatenate([r1, r2, r1, r3, r2, r1], axis=0),
        )
        if k < 2:
            right_kv[k] = right
        else:
            right_out[...] = right
        high, low = split2(right)
        packed.append(jnp.concatenate([high, high, low, jnp.zeros_like(high)], axis=0))
    stores = []
    for j in range(8):
        dh, i = j // 4, j % 4
        bgkv, bekv, bgout, beout = halves[dh]
        for s in range(2):
            merged = bgkv[i, s].astype(F32) + bekv[i, s].astype(F32)
            nkv[j, s] = (merged - dot(ortho[dh][i, s, :CH], packed[s])).astype(BF16)
            rows = slice(s * HALF, (s + 1) * HALF)
            merged = bgout[i, rows].astype(F32) + beout[i, rows].astype(F32)
            nout[j, rows] = (merged - dot(ortho[dh][i, s, CH:], packed[2])).astype(BF16)
        t = my_chunk(dh, i // 2, i % 2)
        rows = pl.ds(pl.multiple_of(t * CH, CH), CH)
        orows = pl.ds(pl.multiple_of(t * OCH, OCH), OCH)
        stores.append(pltpu.make_async_copy(nkv.at[j], new_kv.at[0, :, rows, :], nsems.at[j, 0]))
        stores.append(pltpu.make_async_copy(nout.at[j], new_out.at[0, orows, :], nsems.at[j, 1]))
        stores[-2].start()
        stores[-1].start()
    for copy in stores:
        copy.wait()


def errors(bufs, total, w, ortho):
    return pl.pallas_call(
        error_kernel,
        out_shape=(
            jax.ShapeDtypeStruct((2, RANK, COLS), F32),
            jax.ShapeDtypeStruct((RANK, OCOLS), F32),
            jax.ShapeDtypeStruct((1, 2, ROWS, COLS), BF16),
            jax.ShapeDtypeStruct((1, OROWS, OCOLS), BF16),
        ),
        in_specs=[VM] * 12,
        out_specs=(VM, VM, HBM, HBM),
        scratch_shapes=[
            pltpu.VMEM((8, 2, CH, COLS), BF16),
            pltpu.VMEM((8, OCH, OCOLS), BF16),
            pltpu.SemaphoreType.DMA((8, 2)),
        ],
        compiler_params=pltpu.CompilerParams(vmem_limit_bytes=24 * MIB),
        cost_estimate=cost(5),
        name="errors",
    )(*bufs, total, w, *ortho)


X, Y, Z = 0, 1, 2


def on_device(grad_kv, error_kv, grad_out, error_out, basis_kv, basis_out):
    args = (grad_kv, error_kv, grad_out, error_out, jnp.swapaxes(basis_kv, 1, 2), basis_out.T)
    args = [pltpu.with_memory_space_constraint(x, pltpu.HBM) for x in args]
    lead, bufs_other = part(1, args)
    got = send(lead, CORES)
    lead, bufs_own = part(0, args)
    kept = lead + got
    a, b = kept.reshape(2, 2, 2, RANK, WIDE)

    a = a[0] + send(a[1], exchange(X, 0))
    b = b[:, 0] + send(b[:, 1], exchange(Y, 0))
    a = a[0] + send(a[1], exchange(Y, 0))
    b = b[0] + send(b[1], exchange(X, 0))
    for axis_a, axis_b in (((Z, 0), (Y, 1)), ((X, 1), (Z, 0)), ((Z, 1), (X, 1)), ((Y, 1), (Z, 1))):
        a, b = a + send(a, exchange(*axis_a)), b + send(b, exchange(*axis_b))
    a_own = jnp.stack([a, send(a, exchange(Y, 0))])
    b_own = jnp.stack([b, send(b, exchange(X, 0))])
    a_got = send(a_own, exchange(X, 0))
    b_got = send(b_own, exchange(Y, 0))
    a_own2, b_own2 = send(a_own, CORES), send(b_own, CORES)
    sum1, gram1 = right_part(0, bufs_own, (a_own, b_own))
    sum2, gram2 = right_part(0, bufs_other, (a_own2, b_own2))
    a_got, b_got, sum1, sum2 = lax.optimization_barrier((a_got, b_got, sum1, sum2))
    a_got2, b_got2 = send(a_got, CORES), send(b_got, CORES)
    sum3, gram3 = right_part(1, bufs_own, (a_got, b_got))
    total, gram4 = right_part(1, bufs_other, (a_got2, b_got2), (sum1, sum2, sum3))
    w = factor((gram1, gram3, gram2, gram4))
    total = total + send(total, exchange(Y, 0))
    total, w = lax.optimization_barrier((total, w))
    *left, ortho_own = left_part(0, (a_own, a_got, b_own, b_got), w)
    total = total + send(total, exchange(Z, 0))
    total, left = lax.optimization_barrier((total, left))
    left_kv, left_out, ortho_other = left_part(1, (a_own2, a_got2, b_own2, b_got2), w, left)
    total = total + send(total, exchange(Y, 1))
    total, ortho_other = lax.optimization_barrier((total, ortho_other))
    total = total + send(total, exchange(Z, 1))
    right_kv, right_out, new_kv, new_out = errors(
        (*bufs_own, *bufs_other), total, w, (ortho_own, ortho_other)
    )
    return (
        jnp.swapaxes(left_kv, 1, 2),
        left_out.T,
        jnp.swapaxes(right_kv, 1, 2),
        right_out.T,
        new_kv,
        new_out,
    )


def solution(mesh):
    placed = (
        P("dp", None, None, "mp"),
        P("dp", None, None, "mp"),
        P("dp", None, "mp"),
        P("dp", None, "mp"),
        P(None, "mp", None),
        P("mp", None),
    )
    return jax.shard_map(
        on_device,
        mesh=mesh,
        in_specs=placed,
        out_specs=(
            P(),
            P(),
            P(None, "mp", None),
            P("mp", None),
            P("dp", None, None, "mp"),
            P("dp", None, "mp"),
        ),
        check_vma=False,
    )
```

```python
import functools

import jax
import jax.numpy as jnp
from jax import lax
from jax.experimental import pallas as pl
from jax.experimental.pallas import tpu as pltpu
from jax.sharding import PartitionSpec as P

F32, BF16 = jnp.float32, jnp.bfloat16
ROWS, COLS = 8192, 128
OROWS, OCOLS = 4096, 512
RANK = 32
REPLICAS = 16
STEPS = 3
PARTS = 1 << STEPS
CH = ROWS // (2 * PARTS)
OCH = OROWS // (4 * PARTS)
WIDE = CH + OCH
MIB = 1 << 20

X, Y, Z = 0, 1, 2


def other_turn(steps):
    return [(axis, 1 - turn) for axis, turn in steps]


FIRST = [(X, 0), (Y, 0), (Z, 0), (X, 1), (Y, 1), (Z, 1)]
SECOND = [(Y, 0), (Z, 0), (X, 0), (Y, 1), (Z, 1), (X, 1)]
CHAINS = ((FIRST, other_turn(FIRST)), (SECOND, other_turn(SECOND)))
RIGHT = ([(Y, 0), (Z, 0), (Y, 1), (Z, 1)], [(Z, 0), (Y, 0), (Z, 1), (Y, 1)])


def pairs(steps, k):
    out = []
    for i in range(128):
        q, core = [(i // 2) % 4, i // 32, (i // 8) % 4], i % 2
        axis, turn = steps[core][k]
        q[axis] ^= 3 if turn else 1
        out.append((i, ((q[1] * 4 + q[2]) * 4 + q[0]) * 2 + core))
    return out


CORES = [(i, i ^ 1) for i in range(128)]


def send(x, to):
    return lax.ppermute(x, ("dp", "mp"), to)


def my_chunk(chain, dh, i):
    dp, mp = lax.axis_index("dp"), lax.axis_index("mp")
    q = (lax.div(mp, 2), lax.div(dp, 4), lax.rem(dp, 4))
    half = jnp.bitwise_xor(lax.rem(mp, 2), dh)

    def own(step):
        axis, turn = step
        high, low = lax.div(q[axis], 2), lax.rem(q[axis], 2)
        return high if turn else jnp.bitwise_xor(high, low)

    chunk = half
    for k in range(STEPS):
        bit = (1 - half) * own(CHAINS[chain][0][k]) + half * own(CHAINS[chain][1][k])
        chunk = 2 * chunk + jnp.bitwise_xor(bit, (i >> (STEPS - 1 - k)) & 1)
    return chunk


def chunk_rows(chain, dh, i):
    t = my_chunk(chain, dh, i)
    return pl.ds(pl.multiple_of(t * CH, CH), CH), pl.ds(pl.multiple_of(chain * (OROWS // 2) + t * OCH, OCH), OCH)


def dot_nt(a, b):
    return lax.dot_general(a, b, (((1,), (1,)), ((), ())), preferred_element_type=F32)


def dot(a, b):
    return jnp.dot(a, b, preferred_element_type=F32)


def split2(a):
    high = a.astype(BF16)
    return high, (a - high.astype(F32)).astype(BF16)


def split3(a):
    high = a.astype(BF16)
    rest = a - high.astype(F32)
    mid = rest.astype(BF16)
    return high, mid, (rest - mid.astype(F32)).astype(BF16)


def loads(refs, bufs, sems, dh, i):
    gkv, ekv, gout, eout = refs
    bgkv, bekv, bgout, beout = bufs
    copies = []
    for chain in range(2):
        rows, orows = chunk_rows(chain, dh, i)
        for n, (src, dst) in enumerate(
            (
                (gkv.at[0, chain, rows, :], bgkv),
                (ekv.at[0, chain, rows, :], bekv),
                (gout.at[0, orows, :], bgout),
                (eout.at[0, orows, :], beout),
            )
        ):
            copies.append(pltpu.make_async_copy(src, dst.at[i, chain], sems.at[i, chain, n]))
    return copies


HBM = pl.BlockSpec(memory_space=pltpu.HBM)
VM = pl.BlockSpec(memory_space=pltpu.VMEM)


def cost(us):
    return pl.CostEstimate(flops=0, bytes_accessed=int(us * 3_000_000), transcendentals=0)


def part_kernel(dh, gkv, ekv, gout, eout, bkv_hbm, bout_hbm, out, bgkv, bekv, bgout, beout, bkv, bout, bsems, sems):
    basis = [
        pltpu.make_async_copy(bkv_hbm, bkv, bsems.at[0]),
        pltpu.make_async_copy(bout_hbm, bout, bsems.at[1]),
    ]
    copies = [loads((gkv, ekv, gout, eout), (bgkv, bekv, bgout, beout), sems, dh, i) for i in range(PARTS)]
    for copy in basis:
        copy.start()
    for i in range(AHEAD):
        for copy in copies[i]:
            copy.start()
    for copy in basis:
        copy.wait()
    kv = [jnp.concatenate(split3(bkv[a]), axis=0) for a in range(2)]
    kv = [jnp.concatenate([b, b], axis=1) for b in kv]
    ob = jnp.concatenate(split3(bout[...]), axis=0)

    def fold(r):
        return r[:RANK] + (r[RANK : 2 * RANK] + r[2 * RANK :])

    for i in range(PARTS):
        for copy in copies[i]:
            copy.wait()
        if i + AHEAD < PARTS:
            for copy in copies[i + AHEAD]:
                copy.start()
        for a in range(2):
            both = jnp.concatenate([bgkv[i, a], bekv[i, a]], axis=1)
            out[a, i, :, :CH] = fold(dot_nt(kv[a], both))
            out[a, i, :, CH:] = fold(dot_nt(ob, bgout[i, a]) + dot_nt(ob, beout[i, a]))


AHEAD = 3


def part(dh, args):
    kv = jax.ShapeDtypeStruct((PARTS, 2, CH, COLS), BF16)
    out = jax.ShapeDtypeStruct((PARTS, 2, OCH, OCOLS), BF16)
    result = pl.pallas_call(
        functools.partial(part_kernel, dh),
        out_shape=(jax.ShapeDtypeStruct((2, PARTS, RANK, WIDE), F32), kv, kv, out, out),
        in_specs=[HBM] * 6,
        out_specs=(VM,) * 5,
        scratch_shapes=[
            pltpu.VMEM((2, RANK, COLS), F32),
            pltpu.VMEM((RANK, OCOLS), F32),
            pltpu.SemaphoreType.DMA((2,)),
            pltpu.SemaphoreType.DMA((PARTS, 2, 4)),
        ],
        compiler_params=pltpu.CompilerParams(vmem_limit_bytes=20 * MIB),
        cost_estimate=cost(4),
        name="part",
    )(*args)
    return result[0], result[1:]


def tree(items):
    while len(items) > 1:
        items = [a + b for a, b in zip(items[::2], items[1::2])]
    return items[0]


def right_kernel(group, n_before, *refs):
    bgkv, bekv, bgout, beout, lead_a, lead_b = refs[:6]
    before = refs[6 : 6 + n_before]
    right, gram = refs[6 + n_before :]

    def fold(r):
        return r[:RANK] + r[RANK:]

    def square(parts):
        g = dot_nt(jnp.concatenate(parts, axis=0), jnp.concatenate(parts, axis=0))

        def at(i, j):
            return g[i * RANK : (i + 1) * RANK, j * RANK : (j + 1) * RANK]

        return at(0, 0) + ((at(0, 1) + at(1, 0)) + ((at(0, 2) + at(2, 0)) + at(1, 1)))

    sums = [0.0, 0.0, 0.0]
    grams = [[], [], [], []]
    for j in range(PARTS // 2):
        i = group * (PARTS // 2) + j
        for k, x in enumerate((lead_a, lead_b)):
            parts = split3(x[j])
            kv, o = [p[:, :CH] for p in parts], [p[:, CH:] for p in parts]
            grams[k].append(square(kv))
            grams[2 + k].append(square(o))
            both = jnp.concatenate([bgkv[i, k], bekv[i, k]], axis=1)
            r = fold(dot(jnp.concatenate(kv[:2], axis=0), both))
            sums[k] += r[:, :COLS] + r[:, COLS:]
            two = jnp.concatenate(o[:2], axis=0)
            sums[2] += fold(dot(two, bgout[i, k]) + dot(two, beout[i, k]))
    for k in range(4):
        gram[k] = tree(grams[k])
    sums = jnp.concatenate(sums, axis=1)
    for other in before:
        sums += other[...]
    right[...] = sums


def right_part(group, bufs, lead, before=()):
    return pl.pallas_call(
        functools.partial(right_kernel, group, len(before)),
        out_shape=(
            jax.ShapeDtypeStruct((RANK, 2 * COLS + OCOLS), F32),
            jax.ShapeDtypeStruct((4, RANK, RANK), F32),
        ),
        in_specs=[VM] * (6 + len(before)),
        out_specs=(VM, VM),
        compiler_params=pltpu.CompilerParams(vmem_limit_bytes=20 * MIB),
        cost_estimate=cost(2),
        name="right",
    )(*bufs, *lead, *before)


def factor_kernel(g0, g1, g2, g3, out):
    row = lax.broadcasted_iota(jnp.int32, (RANK, 2 * RANK), 0)
    col = lax.broadcasted_iota(jnp.int32, (RANK, 2 * RANK), 1)
    eye = jnp.where(col == row + RANK, 1.0, 0.0).astype(F32)
    gram = [(g0[k] + g1[k]) + (g2[k] + g3[k]) for k in range(4)]
    gram[2] += gram[3]
    wide = [jnp.concatenate([gram[k], jnp.zeros((RANK, RANK), F32)], axis=1) + eye for k in range(3)]
    scale = [jnp.zeros((RANK, 1), F32)] * 3
    below = lax.broadcasted_iota(jnp.int32, (RANK, 1), 0)
    for i in range(RANK):
        for k in range(3):
            pivot = wide[k][i : i + 1, :]
            d = wide[k][i : i + 1, i : i + 1]
            scale[k] = jnp.where(below == i, lax.rsqrt(d), scale[k])
            factor = jnp.where(below > i, wide[k][:, i : i + 1] / d, 0.0)
            wide[k] = wide[k] - factor * pivot
    for k in range(3):
        out[k] = wide[k][:, RANK:] * scale[k]


def factor(grams):
    return pl.pallas_call(
        factor_kernel,
        out_shape=jax.ShapeDtypeStruct((3, RANK, RANK), F32),
        in_specs=[VM] * 4,
        out_specs=VM,
        compiler_params=pltpu.CompilerParams(vmem_limit_bytes=4 * MIB),
        cost_estimate=cost(4),
        name="factor",
    )(*grams)


def left_kernel(dh, *refs):
    a_own, a_got, b_own, b_got, w = refs[:5]
    left_kv, left_out, ortho, bkv, bout, sems = refs[-6:]
    weights = []
    for k in range(3):
        w1, w2, w3 = split3(w[k])
        weights.append(jnp.concatenate([w1, w1, w2, w1, w2, w3], axis=1))

    def apply(k, x):
        l1, l2, l3 = split3(x)
        return dot(weights[k], jnp.concatenate([l1, l2, l1, l3, l2, l1], axis=0))

    def packed(o):
        high = o.astype(BF16).astype(F32)
        rest = o - high
        return jnp.transpose(jnp.concatenate([high, rest, high, jnp.zeros_like(o)], axis=0)).astype(BF16)

    copies = []
    for i in range(PARTS):
        for s, (own, got) in enumerate(((a_own, a_got), (b_own, b_got))):
            x = (own, got)[i // (PARTS // 2)][i % (PARTS // 2)]
            o_kv = apply(s, x[:, :CH])
            o_out = apply(2, x[:, CH:])
            bkv[i, s] = o_kv * (ROWS**0.5)
            bout[i, s] = o_out * (OROWS**0.5)
            ortho[i, s, :CH] = packed(o_kv)
            ortho[i, s, CH:] = packed(o_out)
            rows, orows = chunk_rows(s, dh, i)
            copies.append(pltpu.make_async_copy(bkv.at[i, s], left_kv.at[s, :, rows], sems.at[i, s, 0]))
            copies.append(pltpu.make_async_copy(bout.at[i, s], left_out.at[:, orows], sems.at[i, s, 1]))
            copies[-2].start()
            copies[-1].start()
    for copy in copies:
        copy.wait()


def left_part(dh, lead, w, before=()):
    return pl.pallas_call(
        functools.partial(left_kernel, dh),
        out_shape=(
            jax.ShapeDtypeStruct((2, RANK, ROWS), F32),
            jax.ShapeDtypeStruct((RANK, OROWS), F32),
            jax.ShapeDtypeStruct((PARTS, 2, WIDE, 128), BF16),
        ),
        in_specs=[VM] * 5 + [HBM] * len(before),
        out_specs=(HBM, HBM, VM),
        scratch_shapes=[
            pltpu.VMEM((PARTS, 2, RANK, CH), F32),
            pltpu.VMEM((PARTS, 2, RANK, OCH), F32),
            pltpu.SemaphoreType.DMA((PARTS, 2, 2)),
        ],
        input_output_aliases={5: 0, 6: 1} if before else {},
        compiler_params=pltpu.CompilerParams(vmem_limit_bytes=16 * MIB),
        cost_estimate=cost(2),
        name="left",
    )(*lead, w, *before)


def error_kernel(*refs):
    halves = (refs[:4], refs[4:8])
    total, w, ortho = refs[8], refs[9], refs[10:12]
    right_kv, right_out, new_kv, new_out, nkv, nout, nsems = refs[12:]
    packed = []
    for k, (at, n) in enumerate(((0, COLS), (COLS, COLS), (2 * COLS, OCOLS))):
        w1, w2, w3 = split3(w[k])
        r1, r2, r3 = split3(total[:, at : at + n] * (1.0 / REPLICAS))
        right = dot(
            jnp.concatenate([w1, w1, w2, w1, w2, w3], axis=1),
            jnp.concatenate([r1, r2, r1, r3, r2, r1], axis=0),
        )
        if k < 2:
            right_kv[k] = right
        else:
            right_out[...] = right
        high, low = split2(right)
        packed.append(jnp.concatenate([high, high, low, jnp.zeros_like(high)], axis=0))
    stores = []
    for j in range(2 * PARTS):
        dh, i = j // PARTS, j % PARTS
        bgkv, bekv, bgout, beout = halves[dh]
        for s in range(2):
            merged = bgkv[i, s].astype(F32) + bekv[i, s].astype(F32)
            nkv[j, s] = (merged - dot(ortho[dh][i, s, :CH], packed[s])).astype(BF16)
            merged = bgout[i, s].astype(F32) + beout[i, s].astype(F32)
            nout[j, s] = (merged - dot(ortho[dh][i, s, CH:], packed[2])).astype(BF16)
            rows, orows = chunk_rows(s, dh, i)
            stores.append(pltpu.make_async_copy(nkv.at[j, s], new_kv.at[0, s, rows, :], nsems.at[j, s, 0]))
            stores.append(pltpu.make_async_copy(nout.at[j, s], new_out.at[0, orows, :], nsems.at[j, s, 1]))
            stores[-2].start()
            stores[-1].start()
    for copy in stores:
        copy.wait()


def errors(bufs, total, w, ortho):
    return pl.pallas_call(
        error_kernel,
        out_shape=(
            jax.ShapeDtypeStruct((2, RANK, COLS), F32),
            jax.ShapeDtypeStruct((RANK, OCOLS), F32),
            jax.ShapeDtypeStruct((1, 2, ROWS, COLS), BF16),
            jax.ShapeDtypeStruct((1, OROWS, OCOLS), BF16),
        ),
        in_specs=[VM] * 12,
        out_specs=(VM, VM, HBM, HBM),
        scratch_shapes=[
            pltpu.VMEM((2 * PARTS, 2, CH, COLS), BF16),
            pltpu.VMEM((2 * PARTS, 2, OCH, OCOLS), BF16),
            pltpu.SemaphoreType.DMA((2 * PARTS, 2, 2)),
        ],
        compiler_params=pltpu.CompilerParams(vmem_limit_bytes=24 * MIB),
        cost_estimate=cost(5),
        name="errors",
    )(*bufs, total, w, *ortho)


def on_device(grad_kv, error_kv, grad_out, error_out, basis_kv, basis_out):
    args = (grad_kv, error_kv, grad_out, error_out, jnp.swapaxes(basis_kv, 1, 2), basis_out.T)
    args = [pltpu.with_memory_space_constraint(x, pltpu.HBM) for x in args]
    lead, bufs_other = part(1, args)
    got = send(lead, CORES)
    lead, bufs_own = part(0, args)
    both = list(lead + got)

    for k in range(2 * STEPS):
        for s in range(2):
            x = both[s]
            if k < STEPS:
                n = x.shape[0] // 2
                both[s] = x[:n] + send(x[n:], pairs(CHAINS[s], k))
            else:
                both[s] = x + send(x, pairs(CHAINS[s], k))
    for k in reversed(range(1, STEPS)):
        both = [jnp.concatenate([x, send(x, pairs(CHAINS[s], k))]) for s, x in enumerate(both)]
    own0 = both
    own1 = [send(x, pairs(CHAINS[s], 0)) for s, x in enumerate(both)]
    other0 = [send(x, CORES) for x in own0]
    sum1, gram1 = right_part(0, bufs_own, own0)
    sum2, gram2 = right_part(0, bufs_other, other0)
    own1, sum1, sum2 = lax.optimization_barrier((own1, sum1, sum2))
    other1 = [send(x, CORES) for x in own1]
    sum3, gram3 = right_part(1, bufs_own, own1)
    total, gram4 = right_part(1, bufs_other, other1, (sum1, sum2, sum3))
    own = (own0[0], own1[0], own0[1], own1[1])
    other = (other0[0], other1[0], other0[1], other1[1])
    w = factor((gram1, gram3, gram2, gram4))
    total = total + send(total, pairs(RIGHT, 0))
    total, w = lax.optimization_barrier((total, w))
    *left, ortho_own = left_part(0, own, w)
    total = total + send(total, pairs(RIGHT, 1))
    total, left = lax.optimization_barrier((total, left))
    left_kv, left_out, ortho_other = left_part(1, other, w, left)
    total = total + send(total, pairs(RIGHT, 2))
    total, ortho_other = lax.optimization_barrier((total, ortho_other))
    total = total + send(total, pairs(RIGHT, 3))
    right_kv, right_out, new_kv, new_out = errors((*bufs_own, *bufs_other), total, w, (ortho_own, ortho_other))
    return (
        jnp.swapaxes(left_kv, 1, 2),
        left_out.T,
        jnp.swapaxes(right_kv, 1, 2),
        right_out.T,
        new_kv,
        new_out,
    )


def solution(mesh):
    placed = (
        P("dp", None, None, "mp"),
        P("dp", None, None, "mp"),
        P("dp", None, "mp"),
        P("dp", None, "mp"),
        P(None, "mp", None),
        P("mp", None),
    )
    return jax.shard_map(
        on_device,
        mesh=mesh,
        in_specs=placed,
        out_specs=(
            P(),
            P(),
            P(None, "mp", None),
            P("mp", None),
            P("dp", None, None, "mp"),
            P("dp", None, "mp"),
        ),
        check_vma=False,
    )
```

```python
import functools

import jax
import jax.numpy as jnp
from jax import lax
from jax.experimental import pallas as pl
from jax.experimental.pallas import tpu as pltpu
from jax.sharding import PartitionSpec as P

F32, BF16 = jnp.float32, jnp.bfloat16
ROWS, COLS = 8192, 128
OROWS, OCOLS = 4096, 512
RANK = 32
REPLICAS = 16
STEPS = 3
PARTS = 1 << STEPS
GROUP = PARTS // 2
CH = ROWS // (2 * PARTS)
OCH = OROWS // (4 * PARTS)
WIDE = CH + OCH
MIB = 1 << 20

X, Y, Z = 0, 1, 2


def other_turn(steps):
    return [(axis, 1 - turn) for axis, turn in steps]


FIRST = [(X, 0), (Y, 0), (Z, 0), (X, 1), (Y, 1), (Z, 1)]
SECOND = [(Y, 0), (Z, 0), (X, 0), (Y, 1), (Z, 1), (X, 1)]
CHAINS = ((FIRST, other_turn(FIRST)), (SECOND, other_turn(SECOND)))
RIGHT = ([(Y, 0), (Z, 0), (Y, 1), (Z, 1)], [(Z, 0), (Y, 0), (Z, 1), (Y, 1)])


def pairs(steps, k):
    out = []
    for i in range(128):
        q, core = [(i // 2) % 4, i // 32, (i // 8) % 4], i % 2
        axis, turn = steps[core][k]
        q[axis] ^= 3 if turn else 1
        out.append((i, ((q[1] * 4 + q[2]) * 4 + q[0]) * 2 + core))
    return out


CORES = [(i, i ^ 1) for i in range(128)]


def send(x, to):
    return lax.ppermute(x, ("dp", "mp"), to)


def group_of(chain, dh, d1):
    dp, mp = lax.axis_index("dp"), lax.axis_index("mp")
    q = (lax.div(mp, 2), lax.div(dp, 4), lax.rem(dp, 4))
    half = jnp.bitwise_xor(lax.rem(mp, 2), dh)

    def own(step):
        axis, turn = step
        high, low = lax.div(q[axis], 2), lax.rem(q[axis], 2)
        return high if turn else jnp.bitwise_xor(high, low)

    bits = [(1 - half) * own(CHAINS[chain][0][k]) + half * own(CHAINS[chain][1][k]) for k in range(STEPS)]
    return (2 * half + jnp.bitwise_xor(bits[0], d1)) * GROUP, 2 * bits[1] + bits[2]


def group_rows(chain, first):
    rows = pl.ds(pl.multiple_of(first * CH, CH), GROUP * CH)
    orows = pl.ds(pl.multiple_of(chain * (OROWS // 2) + first * OCH, OCH), GROUP * OCH)
    return rows, orows


def dot_nt(a, b):
    return lax.dot_general(a, b, (((1,), (1,)), ((), ())), preferred_element_type=F32)


def dot(a, b):
    return jnp.dot(a, b, preferred_element_type=F32)


def split2(a):
    high = a.astype(BF16)
    return high, (a - high.astype(F32)).astype(BF16)


def split3(a):
    high = a.astype(BF16)
    rest = a - high.astype(F32)
    mid = rest.astype(BF16)
    return high, mid, (rest - mid.astype(F32)).astype(BF16)


HBM = pl.BlockSpec(memory_space=pltpu.HBM)
VM = pl.BlockSpec(memory_space=pltpu.VMEM)


def cost(us):
    return pl.CostEstimate(flops=0, bytes_accessed=int(us * 3_000_000), transcendentals=0)


def loads(refs, bufs, sems, dh, d1):
    copies = []
    for chain in range(2):
        rows, orows = group_rows(chain, group_of(chain, dh, d1)[0])
        gkv, ekv, gout, eout = refs
        sources = (gkv.at[0, chain, rows, :], ekv.at[0, chain, rows, :], gout.at[0, orows, :], eout.at[0, orows, :])
        for n, (src, dst) in enumerate(zip(sources, bufs)):
            copies.append(pltpu.make_async_copy(src, dst.at[chain], sems.at[chain, n]))
    return copies


def part_kernel(here, then, *refs):
    refs = list(refs)
    take = lambda n: [refs.pop(0) for _ in range(n)]
    hbm, basis = take(4), take(2)
    loaded = here[2]
    bufs = take(4) if loaded else None
    refs = refs[here[3] :]
    outs = take(2)
    bufs = bufs or take(4)
    later = take(4) if then else None
    sems = refs[-1]
    now = [] if loaded else loads(hbm, bufs, sems.at[0], *here[:2])
    after = loads(hbm, later, sems.at[1], *then) if then else []
    if not loaded:
        split_kv, split_out, bkv, bout, bsems = refs[:5]
        first = [
            pltpu.make_async_copy(basis[0], bkv, bsems.at[0]),
            pltpu.make_async_copy(basis[1], bout, bsems.at[1]),
        ]
        for copy in first + now:
            copy.start()
        for copy in first:
            copy.wait()
        for a in range(2):
            b = jnp.concatenate(split3(bkv[a]), axis=0)
            split_kv[a] = jnp.concatenate([b, b], axis=1)
        split_out[...] = jnp.concatenate(split3(bout[...]), axis=0)
        basis = (split_kv, split_out)
    else:
        for copy in after:
            copy.start()
    kv = [basis[0][a] for a in range(2)]
    ob = basis[1][...]

    def fold(r):
        return r[:RANK] + (r[RANK : 2 * RANK] + r[2 * RANK :])

    bgkv, bekv, bgout, beout = bufs
    for chain in range(2):
        if now:
            for copy in now[4 * chain : 4 * chain + 4]:
                copy.wait()
            for copy in after[4 * chain : 4 * chain + 4]:
                copy.start()
        out = outs[chain]
        _, name = group_of(chain, *here[:2])
        for j in range(GROUP):
            rows, orows = slice(j * CH, (j + 1) * CH), slice(j * OCH, (j + 1) * OCH)
            both = jnp.concatenate([bgkv[chain, rows], bekv[chain, rows]], axis=1)
            i = jnp.bitwise_xor(name, j)
            out[i, :, :CH] = fold(dot_nt(kv[chain], both))
            out[i, :, CH:] = fold(dot_nt(ob, bgout[chain, orows]) + dot_nt(ob, beout[chain, orows]))
    for copy in after:
        copy.wait()


def part(here, then, args, basis, bufs=(), after=()):
    lead = jax.ShapeDtypeStruct((GROUP, RANK, WIDE), F32)
    kv = jax.ShapeDtypeStruct((2, GROUP * CH, COLS), BF16)
    out = jax.ShapeDtypeStruct((2, GROUP * OCH, OCOLS), BF16)
    n = (not bufs) + (then is not None)
    split = (jax.ShapeDtypeStruct((2, 3 * RANK, 2 * COLS), BF16), jax.ShapeDtypeStruct((3 * RANK, OCOLS), BF16))
    scratch = [pltpu.VMEM((2, RANK, COLS), F32), pltpu.VMEM((RANK, OCOLS), F32), pltpu.SemaphoreType.DMA((2,))]
    result = pl.pallas_call(
        functools.partial(part_kernel, (*here, bool(bufs), len(after)), then),
        out_shape=(lead, lead) + (kv, kv, out, out) * n + (() if bufs else split),
        in_specs=[HBM] * 4 + [VM if bufs else HBM] * 2 + [VM] * (len(bufs) + len(after)),
        out_specs=(VM,) * (2 + 4 * n + 2 * (not bufs)),
        scratch_shapes=([] if bufs else scratch) + [pltpu.SemaphoreType.DMA((2, 2, 4))],
        compiler_params=pltpu.CompilerParams(vmem_limit_bytes=14 * MIB),
        cost_estimate=cost(PART_US),
        name="part",
    )(*args, *basis, *bufs, *after)
    return result[:2], *[result[2 + 4 * i : 6 + 4 * i] for i in range(n)], *([] if bufs else [result[-2:]])


PART_US = 3


def tree(items):
    while len(items) > 1:
        items = [a + b for a, b in zip(items[::2], items[1::2])]
    return items[0]


def right_kernel(dh, d1, n_before, *refs):
    bgkv, bekv, bgout, beout, lead_a, lead_b = refs[:6]
    before = refs[6 : 6 + n_before]
    right, gram = refs[6 + n_before :]

    def fold(r):
        return r[:RANK] + r[RANK:]

    def square(parts):
        g = dot_nt(jnp.concatenate(parts, axis=0), jnp.concatenate(parts, axis=0))

        def at(i, j):
            return g[i * RANK : (i + 1) * RANK, j * RANK : (j + 1) * RANK]

        return at(0, 0) + ((at(0, 1) + at(1, 0)) + ((at(0, 2) + at(2, 0)) + at(1, 1)))

    sums = [0.0, 0.0, 0.0]
    grams = [[], [], [], []]
    for k, x in enumerate((lead_a, lead_b)):
        _, name = group_of(k, dh, d1)
        for j in range(GROUP):
            parts = split3(x[jnp.bitwise_xor(name, j)])
            kv, o = [p[:, :CH] for p in parts], [p[:, CH:] for p in parts]
            grams[k].append(square(kv))
            grams[2 + k].append(square(o))
            rows, orows = slice(j * CH, (j + 1) * CH), slice(j * OCH, (j + 1) * OCH)
            both = jnp.concatenate([bgkv[k, rows], bekv[k, rows]], axis=1)
            r = fold(dot(jnp.concatenate(kv[:2], axis=0), both))
            sums[k] += r[:, :COLS] + r[:, COLS:]
            two = jnp.concatenate(o[:2], axis=0)
            sums[2] += fold(dot(two, bgout[k, orows]) + dot(two, beout[k, orows]))
    for k in range(4):
        gram[k] = tree(grams[k])
    sums = jnp.concatenate(sums, axis=1)
    for other in before:
        sums += other[...]
    right[...] = sums


def right_part(dh, d1, bufs, lead, before=()):
    return pl.pallas_call(
        functools.partial(right_kernel, dh, d1, len(before)),
        out_shape=(
            jax.ShapeDtypeStruct((RANK, 2 * COLS + OCOLS), F32),
            jax.ShapeDtypeStruct((4, RANK, RANK), F32),
        ),
        in_specs=[VM] * (6 + len(before)),
        out_specs=(VM, VM),
        compiler_params=pltpu.CompilerParams(vmem_limit_bytes=20 * MIB),
        cost_estimate=cost(2),
        name="right",
    )(*bufs, *lead, *before)


def factor_kernel(g0, g1, g2, g3, out):
    row = lax.broadcasted_iota(jnp.int32, (RANK, 2 * RANK), 0)
    col = lax.broadcasted_iota(jnp.int32, (RANK, 2 * RANK), 1)
    eye = jnp.where(col == row + RANK, 1.0, 0.0).astype(F32)
    gram = [(g0[k] + g1[k]) + (g2[k] + g3[k]) for k in range(4)]
    gram[2] += gram[3]
    wide = [jnp.concatenate([gram[k], jnp.zeros((RANK, RANK), F32)], axis=1) + eye for k in range(3)]
    scale = [jnp.zeros((RANK, 1), F32)] * 3
    below = lax.broadcasted_iota(jnp.int32, (RANK, 1), 0)
    for i in range(RANK):
        for k in range(3):
            pivot = wide[k][i : i + 1, :]
            d = wide[k][i : i + 1, i : i + 1]
            scale[k] = jnp.where(below == i, lax.rsqrt(d), scale[k])
            factor = jnp.where(below > i, wide[k][:, i : i + 1] / d, 0.0)
            wide[k] = wide[k] - factor * pivot
    for k in range(3):
        out[k] = wide[k][:, RANK:] * scale[k]


def factor(grams):
    return pl.pallas_call(
        factor_kernel,
        out_shape=jax.ShapeDtypeStruct((3, RANK, RANK), F32),
        in_specs=[VM] * 4,
        out_specs=VM,
        compiler_params=pltpu.CompilerParams(vmem_limit_bytes=4 * MIB),
        cost_estimate=cost(4),
        name="factor",
    )(*grams)


def left_kernel(dh, *refs):
    a_own, a_got, b_own, b_got, w = refs[:5]
    left_kv, left_out, ortho, bkv, bout, sems = refs[-6:]
    weights = []
    for k in range(3):
        w1, w2, w3 = split3(w[k])
        weights.append(jnp.concatenate([w1, w1, w2, w1, w2, w3], axis=1))

    def apply(k, x):
        l1, l2, l3 = split3(x)
        return dot(weights[k], jnp.concatenate([l1, l2, l1, l3, l2, l1], axis=0))

    def packed(o):
        high = o.astype(BF16).astype(F32)
        rest = o - high
        return jnp.transpose(jnp.concatenate([high, rest, high, jnp.zeros_like(o)], axis=0)).astype(BF16)

    copies = []
    for d1 in range(2):
        for s, lead in enumerate(((a_own, a_got)[d1], (b_own, b_got)[d1])):
            first, name = group_of(s, dh, d1)
            for j in range(GROUP):
                x = lead[jnp.bitwise_xor(name, j)]
                o_kv = apply(s, x[:, :CH])
                o_out = apply(2, x[:, CH:])
                bkv[d1, s, :, j * CH : (j + 1) * CH] = o_kv * (ROWS**0.5)
                bout[d1, s, :, j * OCH : (j + 1) * OCH] = o_out * (OROWS**0.5)
                ortho[d1, s, j, :CH] = packed(o_kv)
                ortho[d1, s, j, CH:] = packed(o_out)
            rows, orows = group_rows(s, first)
            copies.append(pltpu.make_async_copy(bkv.at[d1, s], left_kv.at[s, :, rows], sems.at[d1, s, 0]))
            copies.append(pltpu.make_async_copy(bout.at[d1, s], left_out.at[:, orows], sems.at[d1, s, 1]))
            copies[-2].start()
            copies[-1].start()
    for copy in copies:
        copy.wait()


def left_part(dh, lead, w, before=()):
    return pl.pallas_call(
        functools.partial(left_kernel, dh),
        out_shape=(
            jax.ShapeDtypeStruct((2, RANK, ROWS), F32),
            jax.ShapeDtypeStruct((RANK, OROWS), F32),
            jax.ShapeDtypeStruct((2, 2, GROUP, WIDE, 128), BF16),
        ),
        in_specs=[VM] * 5 + [HBM] * len(before),
        out_specs=(HBM, HBM, VM),
        scratch_shapes=[
            pltpu.VMEM((2, 2, RANK, GROUP * CH), F32),
            pltpu.VMEM((2, 2, RANK, GROUP * OCH), F32),
            pltpu.SemaphoreType.DMA((2, 2, 2)),
        ],
        input_output_aliases={5: 0, 6: 1} if before else {},
        compiler_params=pltpu.CompilerParams(vmem_limit_bytes=16 * MIB),
        cost_estimate=cost(2),
        name="left",
    )(*lead, w, *before)


def error_kernel(*refs):
    total, w, ortho = refs[16], refs[17], refs[18:20]
    right_kv, right_out, new_kv, new_out, nkv, nout, nsems = refs[20:]
    packed = []
    for k, (at, n) in enumerate(((0, COLS), (COLS, COLS), (2 * COLS, OCOLS))):
        w1, w2, w3 = split3(w[k])
        r1, r2, r3 = split3(total[:, at : at + n] * (1.0 / REPLICAS))
        right = dot(
            jnp.concatenate([w1, w1, w2, w1, w2, w3], axis=1),
            jnp.concatenate([r1, r2, r1, r3, r2, r1], axis=0),
        )
        if k < 2:
            right_kv[k] = right
        else:
            right_out[...] = right
        high, low = split2(right)
        packed.append(jnp.concatenate([high, high, low, jnp.zeros_like(high)], axis=0))
    stores = []
    for g in range(4):
        dh, d1 = g // 2, g % 2
        bgkv, bekv, bgout, beout = refs[4 * g : 4 * g + 4]
        for s in range(2):
            for j in range(GROUP):
                rows, orows = slice(j * CH, (j + 1) * CH), slice(j * OCH, (j + 1) * OCH)
                merged = bgkv[s, rows].astype(F32) + bekv[s, rows].astype(F32)
                nkv[g, s, rows] = (merged - dot(ortho[dh][d1, s, j, :CH], packed[s])).astype(BF16)
                merged = bgout[s, orows].astype(F32) + beout[s, orows].astype(F32)
                nout[g, s, orows] = (merged - dot(ortho[dh][d1, s, j, CH:], packed[2])).astype(BF16)
            rows, orows = group_rows(s, group_of(s, dh, d1)[0])
            stores.append(pltpu.make_async_copy(nkv.at[g, s], new_kv.at[0, s, rows, :], nsems.at[g, s, 0]))
            stores.append(pltpu.make_async_copy(nout.at[g, s], new_out.at[0, orows, :], nsems.at[g, s, 1]))
            stores[-2].start()
            stores[-1].start()
    for copy in stores:
        copy.wait()


def errors(bufs, total, w, ortho):
    return pl.pallas_call(
        error_kernel,
        out_shape=(
            jax.ShapeDtypeStruct((2, RANK, COLS), F32),
            jax.ShapeDtypeStruct((RANK, OCOLS), F32),
            jax.ShapeDtypeStruct((1, 2, ROWS, COLS), BF16),
            jax.ShapeDtypeStruct((1, OROWS, OCOLS), BF16),
        ),
        in_specs=[VM] * 20,
        out_specs=(VM, VM, HBM, HBM),
        scratch_shapes=[
            pltpu.VMEM((4, 2, GROUP * CH, COLS), BF16),
            pltpu.VMEM((4, 2, GROUP * OCH, OCOLS), BF16),
            pltpu.SemaphoreType.DMA((4, 2, 2)),
        ],
        compiler_params=pltpu.CompilerParams(vmem_limit_bytes=24 * MIB),
        cost_estimate=cost(5),
        name="errors",
    )(*bufs, total, w, *ortho)


def on_device(grad_kv, error_kv, grad_out, error_out, basis_kv, basis_out):
    args = (grad_kv, error_kv, grad_out, error_out, jnp.swapaxes(basis_kv, 1, 2), basis_out.T)
    *args, bkv, bout = [pltpu.with_memory_space_constraint(x, pltpu.HBM) for x in args]
    far, bufs_far1, bufs_near1, basis = part((1, 1), (0, 1), args, (bkv, bout))
    far = [send(x, CORES) for x in far]
    near, bufs_far0 = part((0, 1), (1, 0), args, basis, bufs_near1)
    sent = [x + y for x, y in zip(near, far)]
    got = [send(x, pairs(CHAINS[s], 0)) for s, x in enumerate(sent)]
    far, bufs_near0 = part((1, 0), (0, 0), args, basis, bufs_far0, sent)
    far = [send(x, CORES) for x in far]
    (near,) = part((0, 0), None, args, basis, bufs_near0, got[1:])
    both = [(x + y) + z for x, y, z in zip(near, far, got)]

    for k in range(1, 2 * STEPS):
        for s in range(2):
            x = both[s]
            if k < STEPS:
                n = x.shape[0] // 2
                both[s] = x[:n] + send(x[n:], pairs(CHAINS[s], k))
            else:
                both[s] = x + send(x, pairs(CHAINS[s], k))
    for k in reversed(range(1, STEPS)):
        both = [jnp.concatenate([x, send(x, pairs(CHAINS[s], k))]) for s, x in enumerate(both)]
    own0 = both
    own1 = [send(x, pairs(CHAINS[s], 0)) for s, x in enumerate(both)]
    other0 = [send(x, CORES) for x in own0]
    sum1, gram1 = right_part(0, 0, bufs_near0, own0)
    sum2, gram2 = right_part(1, 0, bufs_far0, other0)
    own1, sum1, sum2 = lax.optimization_barrier((own1, sum1, sum2))
    other1 = [send(x, CORES) for x in own1]
    sum3, gram3 = right_part(0, 1, bufs_near1, own1)
    total, gram4 = right_part(1, 1, bufs_far1, other1, (sum1, sum2, sum3))
    own = (own0[0], own1[0], own0[1], own1[1])
    other = (other0[0], other1[0], other0[1], other1[1])
    w = factor((gram1, gram3, gram2, gram4))
    total = total + send(total, pairs(RIGHT, 0))
    total, w = lax.optimization_barrier((total, w))
    *left, ortho_own = left_part(0, own, w)
    total = total + send(total, pairs(RIGHT, 1))
    total, left = lax.optimization_barrier((total, left))
    left_kv, left_out, ortho_other = left_part(1, other, w, left)
    total = total + send(total, pairs(RIGHT, 2))
    total, ortho_other = lax.optimization_barrier((total, ortho_other))
    total = total + send(total, pairs(RIGHT, 3))
    right_kv, right_out, new_kv, new_out = errors(
        (*bufs_near0, *bufs_near1, *bufs_far0, *bufs_far1), total, w, (ortho_own, ortho_other)
    )
    return (
        jnp.swapaxes(left_kv, 1, 2),
        left_out.T,
        jnp.swapaxes(right_kv, 1, 2),
        right_out.T,
        new_kv,
        new_out,
    )


def solution(mesh):
    placed = (
        P("dp", None, None, "mp"),
        P("dp", None, None, "mp"),
        P("dp", None, "mp"),
        P("dp", None, "mp"),
        P(None, "mp", None),
        P("mp", None),
    )
    return jax.shard_map(
        on_device,
        mesh=mesh,
        in_specs=placed,
        out_specs=(
            P(),
            P(),
            P(None, "mp", None),
            P("mp", None),
            P("dp", None, None, "mp"),
            P("dp", None, "mp"),
        ),
        check_vma=False,
    )
```

```python
import functools

import jax
import jax.numpy as jnp
from jax import lax
from jax.experimental import pallas as pl
from jax.experimental.pallas import tpu as pltpu
from jax.sharding import PartitionSpec as P

F32, BF16 = jnp.float32, jnp.bfloat16
ROWS, COLS = 8192, 128
OROWS, OCOLS = 4096, 512
RANK = 32
REPLICAS = 16
STEPS = 3
PARTS = 1 << STEPS
GROUP = PARTS // 2
CH = ROWS // (2 * PARTS)
OCH = OROWS // (4 * PARTS)
WIDE = CH + OCH
MIB = 1 << 20

X, Y, Z = 0, 1, 2


def other_turn(steps):
    return [(axis, 1 - turn) for axis, turn in steps]


FIRST = [(X, 0), (Y, 0), (Z, 0), (X, 1), (Y, 1), (Z, 1)]
SECOND = [(Y, 0), (Z, 0), (X, 0), (Y, 1), (Z, 1), (X, 1)]
CHAINS = ((FIRST, other_turn(FIRST)), (SECOND, other_turn(SECOND)))
RIGHT = ([(Y, 0), (Z, 0), (Y, 1), (Z, 1)], [(Z, 0), (Y, 0), (Z, 1), (Y, 1)])


def pairs(steps, k):
    out = []
    for i in range(128):
        q, core = [(i // 2) % 4, i // 32, (i // 8) % 4], i % 2
        axis, turn = steps[core][k]
        q[axis] ^= 3 if turn else 1
        out.append((i, ((q[1] * 4 + q[2]) * 4 + q[0]) * 2 + core))
    return out


CORES = [(i, i ^ 1) for i in range(128)]


def send(x, to):
    return lax.ppermute(x, ("dp", "mp"), to)


def group_of(chain, dh, d1):
    dp, mp = lax.axis_index("dp"), lax.axis_index("mp")
    q = (lax.div(mp, 2), lax.div(dp, 4), lax.rem(dp, 4))
    half = jnp.bitwise_xor(lax.rem(mp, 2), dh)

    def own(step):
        axis, turn = step
        high, low = lax.div(q[axis], 2), lax.rem(q[axis], 2)
        return high if turn else jnp.bitwise_xor(high, low)

    bits = [(1 - half) * own(CHAINS[chain][0][k]) + half * own(CHAINS[chain][1][k]) for k in range(STEPS)]
    return (2 * half + jnp.bitwise_xor(bits[0], d1)) * GROUP, 2 * bits[1] + bits[2]


def group_rows(chain, first):
    rows = pl.ds(pl.multiple_of(first * CH, CH), GROUP * CH)
    orows = pl.ds(pl.multiple_of(chain * (OROWS // 2) + first * OCH, OCH), GROUP * OCH)
    return rows, orows


def dot_nt(a, b):
    return lax.dot_general(a, b, (((1,), (1,)), ((), ())), preferred_element_type=F32)


def dot(a, b):
    return jnp.dot(a, b, preferred_element_type=F32)


def split2(a):
    high = a.astype(BF16)
    return high, (a - high.astype(F32)).astype(BF16)


def split3(a):
    high = a.astype(BF16)
    rest = a - high.astype(F32)
    mid = rest.astype(BF16)
    return high, mid, (rest - mid.astype(F32)).astype(BF16)


HBM = pl.BlockSpec(memory_space=pltpu.HBM)
VM = pl.BlockSpec(memory_space=pltpu.VMEM)


def cost(us):
    return pl.CostEstimate(flops=0, bytes_accessed=int(us * 3_000_000), transcendentals=0)


KV_ROWS = jax.ShapeDtypeStruct((GROUP * CH, COLS), BF16)
OUT_ROWS = jax.ShapeDtypeStruct((GROUP * OCH, OCOLS), BF16)
ROW_SHAPES = [KV_ROWS, KV_ROWS, OUT_ROWS, OUT_ROWS]


def loads(refs, bufs, sems, chain, group):
    rows, orows = group_rows(chain, group_of(chain, *group)[0])
    gkv, ekv, gout, eout = refs
    sources = (gkv.at[0, chain, rows, :], ekv.at[0, chain, rows, :], gout.at[0, orows, :], eout.at[0, orows, :])
    return [pltpu.make_async_copy(src, dst, sems.at[n]) for n, (src, dst) in enumerate(zip(sources, bufs))]


def part_kernel(group, given, ahead, n_after, first, *refs):
    refs = list(refs)
    take = lambda n: [refs.pop(0) for _ in range(n)]
    hbm, basis = take(4), take(2)
    bufs = {chain: take(4) for chain in given}
    take(n_after)
    outs = take(2)
    here = [chain for chain in range(2) if chain not in given]
    for chain in here:
        bufs[chain] = take(4)
    later = [take(4) for _ in ahead]
    sems = refs[-1]
    now = {chain: loads(hbm, bufs[chain], sems.at[chain], chain, group) for chain in here}
    after = [c for n, (chain, g) in enumerate(ahead) for c in loads(hbm, later[n], sems.at[2 + n], chain, g)]
    if first:
        split_kv, split_out, bkv, bout, bsems = refs[:5]
        copies = [
            pltpu.make_async_copy(basis[0], bkv, bsems.at[0]),
            pltpu.make_async_copy(basis[1], bout, bsems.at[1]),
        ]
        for copy in copies:
            copy.start()
    for chain in here:
        for copy in now[chain]:
            copy.start()
    if not first:
        for copy in after:
            copy.start()
    if first:
        for copy in copies:
            copy.wait()
        for a in range(2):
            b = jnp.concatenate(split3(bkv[a]), axis=0)
            split_kv[a] = jnp.concatenate([b, b], axis=1)
        split_out[...] = jnp.concatenate(split3(bout[...]), axis=0)
        basis = (split_kv, split_out)

    def fold(r):
        return r[:RANK] + (r[RANK : 2 * RANK] + r[2 * RANK :])

    for chain in [*given, *here]:
        for copy in now.get(chain, []):
            copy.wait()
        if first and chain == here[0]:
            for copy in after:
                copy.start()
        gkv, ekv, gout, eout = bufs[chain]
        _, name = group_of(chain, *group)
        for j in range(GROUP):
            rows, orows = slice(j * CH, (j + 1) * CH), slice(j * OCH, (j + 1) * OCH)
            i = jnp.bitwise_xor(name, j)
            both = jnp.concatenate([gkv[rows], ekv[rows]], axis=1)
            outs[chain][i, :, :CH] = fold(dot_nt(basis[0][chain], both))
            outs[chain][i, :, CH:] = fold(dot_nt(basis[1][...], gout[orows]) + dot_nt(basis[1][...], eout[orows]))
    for copy in after:
        copy.wait()


def part(group, args, basis, bufs, ahead=(), after=(), first=False):
    given = [chain for chain in range(2) if (chain, group) in bufs]
    loaded = [(chain, group) for chain in range(2) if chain not in given] + list(ahead)
    shapes = [jax.ShapeDtypeStruct((GROUP, RANK, WIDE), F32)] * 2 + ROW_SHAPES * len(loaded)
    scratch = [pltpu.SemaphoreType.DMA((2 + len(ahead), 4))]
    if first:
        shapes.append(jax.ShapeDtypeStruct((2, 3 * RANK, 2 * COLS), BF16))
        shapes.append(jax.ShapeDtypeStruct((3 * RANK, OCOLS), BF16))
        scratch = [pltpu.VMEM((2, RANK, COLS), F32), pltpu.VMEM((RANK, OCOLS), F32), pltpu.SemaphoreType.DMA((2,))] + scratch
    operands = [x for chain in given for x in bufs[chain, group]]
    result = pl.pallas_call(
        functools.partial(part_kernel, group, given, ahead, len(after), first),
        out_shape=shapes,
        in_specs=[HBM] * 4 + [HBM if first else VM] * 2 + [VM] * (len(operands) + len(after)),
        out_specs=[VM] * len(shapes),
        scratch_shapes=scratch,
        compiler_params=pltpu.CompilerParams(vmem_limit_bytes=16 * MIB),
        cost_estimate=cost(3),
        name="part",
    )(*args, *basis, *operands, *after)
    for n, key in enumerate(loaded):
        bufs[key] = tuple(result[2 + 4 * n : 6 + 4 * n])
    return result[:2], result[2 + 4 * len(loaded) :]


def tree(items):
    while len(items) > 1:
        items = [a + b for a, b in zip(items[::2], items[1::2])]
    return items[0]


def right_kernel(chain, group, n_before, last, *refs):
    bufs, x = refs[:4], refs[4]
    before = refs[5 : 5 + n_before]
    keys = refs[5 + n_before] if last else None
    right, gram = refs[-2:]

    def fold(r):
        return r[:RANK] + r[RANK:]

    def square(parts):
        g = dot_nt(jnp.concatenate(parts, axis=0), jnp.concatenate(parts, axis=0))

        def at(i, j):
            return g[i * RANK : (i + 1) * RANK, j * RANK : (j + 1) * RANK]

        return at(0, 0) + ((at(0, 1) + at(1, 0)) + ((at(0, 2) + at(2, 0)) + at(1, 1)))

    sums = [0.0, 0.0]
    grams = [[], []]
    _, name = group_of(chain, *group)
    for j in range(GROUP):
        parts = split3(x[jnp.bitwise_xor(name, j)])
        rows, orows = slice(j * CH, (j + 1) * CH), slice(j * OCH, (j + 1) * OCH)
        kv, o = [p[:, :CH] for p in parts], [p[:, CH:] for p in parts]
        grams[0].append(square(kv))
        grams[1].append(square(o))
        both = jnp.concatenate([bufs[0][rows], bufs[1][rows]], axis=1)
        r = fold(dot(jnp.concatenate(kv[:2], axis=0), both))
        sums[0] += r[:, :COLS] + r[:, COLS:]
        two = jnp.concatenate(o[:2], axis=0)
        sums[1] += fold(dot(two, bufs[2][orows]) + dot(two, bufs[3][orows]))
    for k in range(2):
        gram[k] = tree(grams[k])
    sums = jnp.concatenate(sums, axis=1)
    for other in before:
        sums += other[...]
    if last:
        right[:, :COLS] = keys[:, :COLS]
        right[:, COLS : 2 * COLS] = sums[:, :COLS]
        right[:, 2 * COLS :] = keys[:, COLS:] + sums[:, COLS:]
    else:
        right[...] = sums


def right_part(chain, group, bufs, lead, before=(), keys=None):
    last = keys is not None
    width = 2 * COLS + OCOLS if last else COLS + OCOLS
    operands = (*bufs[chain, group], lead, *before, *([keys] if last else []))
    return pl.pallas_call(
        functools.partial(right_kernel, chain, group, len(before), last),
        out_shape=(
            jax.ShapeDtypeStruct((RANK, width), F32),
            jax.ShapeDtypeStruct((2, RANK, RANK), F32),
        ),
        in_specs=[VM] * len(operands),
        out_specs=(VM, VM),
        compiler_params=pltpu.CompilerParams(vmem_limit_bytes=16 * MIB),
        cost_estimate=cost(1),
        name="right",
    )(*operands)


def factor_kernel(a0, a1, a2, a3, b0, b1, b2, b3, out):
    row = lax.broadcasted_iota(jnp.int32, (RANK, 2 * RANK), 0)
    col = lax.broadcasted_iota(jnp.int32, (RANK, 2 * RANK), 1)
    eye = jnp.where(col == row + RANK, 1.0, 0.0).astype(F32)
    keys, outs_a = [(a0[k] + a1[k]) + (a2[k] + a3[k]) for k in range(2)]
    values, outs_b = [(b0[k] + b1[k]) + (b2[k] + b3[k]) for k in range(2)]
    gram = [keys, values, outs_a + outs_b]
    wide = [jnp.concatenate([gram[k], jnp.zeros((RANK, RANK), F32)], axis=1) + eye for k in range(3)]
    scale = [jnp.zeros((RANK, 1), F32)] * 3
    below = lax.broadcasted_iota(jnp.int32, (RANK, 1), 0)
    for i in range(RANK):
        for k in range(3):
            pivot = wide[k][i : i + 1, :]
            d = wide[k][i : i + 1, i : i + 1]
            scale[k] = jnp.where(below == i, lax.rsqrt(d), scale[k])
            factor = jnp.where(below > i, wide[k][:, i : i + 1] / d, 0.0)
            wide[k] = wide[k] - factor * pivot
    for k in range(3):
        out[k] = wide[k][:, RANK:] * scale[k]


def factor(grams):
    return pl.pallas_call(
        factor_kernel,
        out_shape=jax.ShapeDtypeStruct((3, RANK, RANK), F32),
        in_specs=[VM] * 8,
        out_specs=VM,
        compiler_params=pltpu.CompilerParams(vmem_limit_bytes=4 * MIB),
        cost_estimate=cost(4),
        name="factor",
    )(*grams)


def left_kernel(dh, *refs):
    a_own, a_got, b_own, b_got, w = refs[:5]
    left_kv, left_out, ortho, bkv, bout, sems = refs[-6:]
    weights = []
    for k in range(3):
        w1, w2, w3 = split3(w[k])
        weights.append(jnp.concatenate([w1, w1, w2, w1, w2, w3], axis=1))

    def apply(k, x):
        l1, l2, l3 = split3(x)
        return dot(weights[k], jnp.concatenate([l1, l2, l1, l3, l2, l1], axis=0))

    def packed(o):
        high = o.astype(BF16).astype(F32)
        rest = o - high
        return jnp.transpose(jnp.concatenate([high, rest, high, jnp.zeros_like(o)], axis=0)).astype(BF16)

    copies = []
    for d1 in range(2):
        for s, lead in enumerate(((a_own, a_got)[d1], (b_own, b_got)[d1])):
            first, name = group_of(s, dh, d1)
            for j in range(GROUP):
                x = lead[jnp.bitwise_xor(name, j)]
                o_kv = apply(s, x[:, :CH])
                o_out = apply(2, x[:, CH:])
                bkv[d1, s, :, j * CH : (j + 1) * CH] = o_kv * (ROWS**0.5)
                bout[d1, s, :, j * OCH : (j + 1) * OCH] = o_out * (OROWS**0.5)
                ortho[d1, s, j, :CH] = packed(o_kv)
                ortho[d1, s, j, CH:] = packed(o_out)
            rows, orows = group_rows(s, first)
            copies.append(pltpu.make_async_copy(bkv.at[d1, s], left_kv.at[s, :, rows], sems.at[d1, s, 0]))
            copies.append(pltpu.make_async_copy(bout.at[d1, s], left_out.at[:, orows], sems.at[d1, s, 1]))
            copies[-2].start()
            copies[-1].start()
    for copy in copies:
        copy.wait()


def left_part(dh, lead, w, before=()):
    return pl.pallas_call(
        functools.partial(left_kernel, dh),
        out_shape=(
            jax.ShapeDtypeStruct((2, RANK, ROWS), F32),
            jax.ShapeDtypeStruct((RANK, OROWS), F32),
            jax.ShapeDtypeStruct((2, 2, GROUP, WIDE, 128), BF16),
        ),
        in_specs=[VM] * 5 + [HBM] * len(before),
        out_specs=(HBM, HBM, VM),
        scratch_shapes=[
            pltpu.VMEM((2, 2, RANK, GROUP * CH), F32),
            pltpu.VMEM((2, 2, RANK, GROUP * OCH), F32),
            pltpu.SemaphoreType.DMA((2, 2, 2)),
        ],
        input_output_aliases={5: 0, 6: 1} if before else {},
        compiler_params=pltpu.CompilerParams(vmem_limit_bytes=16 * MIB),
        cost_estimate=cost(2),
        name="left",
    )(*lead, w, *before)


def error_kernel(*refs):
    total, w, ortho = refs[32], refs[33], refs[34:36]
    right_kv, right_out, new_kv, new_out, nkv, nout, nsems = refs[36:]
    packed = []
    for k, (at, n) in enumerate(((0, COLS), (COLS, COLS), (2 * COLS, OCOLS))):
        w1, w2, w3 = split3(w[k])
        r1, r2, r3 = split3(total[:, at : at + n] * (1.0 / REPLICAS))
        right = dot(
            jnp.concatenate([w1, w1, w2, w1, w2, w3], axis=1),
            jnp.concatenate([r1, r2, r1, r3, r2, r1], axis=0),
        )
        if k < 2:
            right_kv[k] = right
        else:
            right_out[...] = right
        high, low = split2(right)
        packed.append(jnp.concatenate([high, high, low, jnp.zeros_like(high)], axis=0))
    stores = []
    for g, (dh, d1) in enumerate(GROUPS):
        for s in range(2):
            gkv, ekv, gout, eout = refs[8 * g + 4 * s : 8 * g + 4 * s + 4]
            for j in range(GROUP):
                at, oat = slice(j * CH, (j + 1) * CH), slice(j * OCH, (j + 1) * OCH)
                merged = gkv[at].astype(F32) + ekv[at].astype(F32)
                nkv[g, s, at] = (merged - dot(ortho[dh][d1, s, j, :CH], packed[s])).astype(BF16)
                merged = gout[oat].astype(F32) + eout[oat].astype(F32)
                nout[g, s, oat] = (merged - dot(ortho[dh][d1, s, j, CH:], packed[2])).astype(BF16)
            rows, orows = group_rows(s, group_of(s, dh, d1)[0])
            stores.append(pltpu.make_async_copy(nkv.at[g, s], new_kv.at[0, s, rows, :], nsems.at[g, s, 0]))
            stores.append(pltpu.make_async_copy(nout.at[g, s], new_out.at[0, orows, :], nsems.at[g, s, 1]))
            stores[-2].start()
            stores[-1].start()
    for copy in stores:
        copy.wait()


GROUPS = ((0, 0), (0, 1), (1, 0), (1, 1))


def errors(bufs, total, w, ortho):
    bufs = [x for group in GROUPS for chain in range(2) for x in bufs[chain, group]]
    return pl.pallas_call(
        error_kernel,
        out_shape=(
            jax.ShapeDtypeStruct((2, RANK, COLS), F32),
            jax.ShapeDtypeStruct((RANK, OCOLS), F32),
            jax.ShapeDtypeStruct((1, 2, ROWS, COLS), BF16),
            jax.ShapeDtypeStruct((1, OROWS, OCOLS), BF16),
        ),
        in_specs=[VM] * 36,
        out_specs=(VM, VM, HBM, HBM),
        scratch_shapes=[
            pltpu.VMEM((4, 2, GROUP * CH, COLS), BF16),
            pltpu.VMEM((4, 2, GROUP * OCH, OCOLS), BF16),
            pltpu.SemaphoreType.DMA((4, 2, 2)),
        ],
        compiler_params=pltpu.CompilerParams(vmem_limit_bytes=24 * MIB),
        cost_estimate=cost(5),
        name="errors",
    )(*bufs, total, w, *ortho)


def on_device(grad_kv, error_kv, grad_out, error_out, basis_kv, basis_out):
    args = (grad_kv, error_kv, grad_out, error_out, jnp.swapaxes(basis_kv, 1, 2), basis_out.T)
    *args, bkv, bout = [pltpu.with_memory_space_constraint(x, pltpu.HBM) for x in args]
    near0, near1, far0, far1 = GROUPS
    bufs = {}
    far, basis = part(far1, args, (bkv, bout), bufs, [(0, near1)], first=True)
    far = [send(x, CORES) for x in far]
    near, _ = part(near1, args, basis, bufs, [(0, far0)])
    sent = [x + y for x, y in zip(near, far)]
    got = [send(x, pairs(CHAINS[s], 0)) for s, x in enumerate(sent)]
    far, _ = part(far0, args, basis, bufs, [(0, near0), (1, near0)], after=sent)
    far = [send(x, CORES) for x in far]
    near, _ = part(near0, args, basis, bufs, after=got[1:])
    both = [(x + y) + z for x, y, z in zip(near, far, got)]

    for k in range(1, 2 * STEPS):
        for s in range(2):
            x = both[s]
            if k < STEPS:
                n = x.shape[0] // 2
                both[s] = x[:n] + send(x[n:], pairs(CHAINS[s], k))
            else:
                both[s] = x + send(x, pairs(CHAINS[s], k))
    for k in reversed(range(1, STEPS)):
        both = [jnp.concatenate([x, send(x, pairs(CHAINS[s], k))]) for s, x in enumerate(both)]
    own0 = both
    own1 = [send(x, pairs(CHAINS[s], 0)) for s, x in enumerate(both)]
    other0 = [send(x, CORES) for x in own0]
    other1, grams, total = [], [], None
    for s in range(2):
        sum1, gram1 = right_part(s, near0, bufs, own0[s])
        sum2, gram2 = right_part(s, far0, bufs, other0[s])
        own1[s], sum1, sum2 = lax.optimization_barrier((own1[s], sum1, sum2))
        other1.append(send(own1[s], CORES))
        sum3, gram3 = right_part(s, near1, bufs, own1[s])
        total, gram4 = right_part(s, far1, bufs, other1[s], (sum1, sum2, sum3), total)
        grams += [gram1, gram3, gram2, gram4]
    own = (own0[0], own1[0], own0[1], own1[1])
    other = (other0[0], other1[0], other0[1], other1[1])
    w = factor(grams)
    total = total + send(total, pairs(RIGHT, 0))
    total, w = lax.optimization_barrier((total, w))
    *left, ortho_own = left_part(0, own, w)
    total = total + send(total, pairs(RIGHT, 1))
    total, left = lax.optimization_barrier((total, left))
    left_kv, left_out, ortho_other = left_part(1, other, w, left)
    total = total + send(total, pairs(RIGHT, 2))
    total, ortho_other = lax.optimization_barrier((total, ortho_other))
    total = total + send(total, pairs(RIGHT, 3))
    right_kv, right_out, new_kv, new_out = errors(bufs, total, w, (ortho_own, ortho_other))
    return (
        jnp.swapaxes(left_kv, 1, 2),
        left_out.T,
        jnp.swapaxes(right_kv, 1, 2),
        right_out.T,
        new_kv,
        new_out,
    )


def solution(mesh):
    placed = (
        P("dp", None, None, "mp"),
        P("dp", None, None, "mp"),
        P("dp", None, "mp"),
        P("dp", None, "mp"),
        P(None, "mp", None),
        P("mp", None),
    )
    return jax.shard_map(
        on_device,
        mesh=mesh,
        in_specs=placed,
        out_specs=(
            P(),
            P(),
            P(None, "mp", None),
            P("mp", None),
            P("dp", None, None, "mp"),
            P("dp", None, "mp"),
        ),
        check_vma=False,
    )
```

```python
import functools

import jax
import jax.numpy as jnp
from jax import lax
from jax.experimental import pallas as pl
from jax.experimental.pallas import tpu as pltpu
from jax.sharding import PartitionSpec as P

F32, BF16 = jnp.float32, jnp.bfloat16
ROWS, COLS = 8192, 128
OROWS, OCOLS = 4096, 512
RANK = 32
REPLICAS = 16
STEPS = 3
PARTS = 1 << STEPS
GROUP = PARTS // 2
CH = ROWS // (2 * PARTS)
OCH = OROWS // (4 * PARTS)
WIDE = CH + OCH
MIB = 1 << 20

X, Y, Z = 0, 1, 2


def other_turn(steps):
    return [(axis, 1 - turn) for axis, turn in steps]


FIRST = [(X, 0), (Y, 0), (Z, 0), (X, 1), (Y, 1), (Z, 1)]
SECOND = [(Y, 0), (Z, 0), (X, 0), (Y, 1), (Z, 1), (X, 1)]
CHAINS = ((FIRST, other_turn(FIRST)), (SECOND, other_turn(SECOND)))
RIGHT = ([(Y, 0), (Z, 0), (Y, 1), (Z, 1)], [(Z, 0), (Y, 0), (Z, 1), (Y, 1)])


def pairs(steps, k):
    out = []
    for i in range(128):
        q, core = [(i // 2) % 4, i // 32, (i // 8) % 4], i % 2
        axis, turn = steps[core][k]
        q[axis] ^= 3 if turn else 1
        out.append((i, ((q[1] * 4 + q[2]) * 4 + q[0]) * 2 + core))
    return out


CORES = [(i, i ^ 1) for i in range(128)]


def send(x, to):
    return lax.ppermute(x, ("dp", "mp"), to)


def group_of(chain, dh, d1):
    dp, mp = lax.axis_index("dp"), lax.axis_index("mp")
    q = (lax.div(mp, 2), lax.div(dp, 4), lax.rem(dp, 4))
    half = jnp.bitwise_xor(lax.rem(mp, 2), dh)

    def own(step):
        axis, turn = step
        high, low = lax.div(q[axis], 2), lax.rem(q[axis], 2)
        return high if turn else jnp.bitwise_xor(high, low)

    bits = [(1 - half) * own(CHAINS[chain][0][k]) + half * own(CHAINS[chain][1][k]) for k in range(STEPS)]
    return (2 * half + jnp.bitwise_xor(bits[0], d1)) * GROUP, 2 * bits[1] + bits[2]


def group_rows(chain, first):
    rows = pl.ds(pl.multiple_of(first * CH, CH), GROUP * CH)
    orows = pl.ds(pl.multiple_of(chain * (OROWS // 2) + first * OCH, OCH), GROUP * OCH)
    return rows, orows


def dot_nt(a, b):
    return lax.dot_general(a, b, (((1,), (1,)), ((), ())), preferred_element_type=F32)


def dot(a, b):
    return jnp.dot(a, b, preferred_element_type=F32)


def split2(a):
    high = a.astype(BF16)
    return high, (a - high.astype(F32)).astype(BF16)


def split3(a):
    high = a.astype(BF16)
    rest = a - high.astype(F32)
    mid = rest.astype(BF16)
    return high, mid, (rest - mid.astype(F32)).astype(BF16)


HBM = pl.BlockSpec(memory_space=pltpu.HBM)
VM = pl.BlockSpec(memory_space=pltpu.VMEM)


def cost(us):
    return pl.CostEstimate(flops=0, bytes_accessed=int(us * 3_000_000), transcendentals=0)


KV_ROWS = jax.ShapeDtypeStruct((GROUP * CH, COLS), BF16)
OUT_ROWS = jax.ShapeDtypeStruct((GROUP * OCH, OCOLS), BF16)
ROW_SHAPES = [KV_ROWS, KV_ROWS, OUT_ROWS, OUT_ROWS]


def loads(refs, bufs, sems, chain, group):
    rows, orows = group_rows(chain, group_of(chain, *group)[0])
    gkv, ekv, gout, eout = refs
    sources = (gkv.at[0, chain, rows, :], ekv.at[0, chain, rows, :], gout.at[0, orows, :], eout.at[0, orows, :])
    return [pltpu.make_async_copy(src, dst, sems.at[n]) for n, (src, dst) in enumerate(zip(sources, bufs))]


def part_kernel(group, given, ahead, n_after, first, *refs):
    refs = list(refs)
    take = lambda n: [refs.pop(0) for _ in range(n)]
    hbm, basis = take(4), take(2)
    bufs = {chain: take(4) for chain in given}
    take(n_after)
    outs = take(2)
    here = [chain for chain in range(2) if chain not in given]
    for chain in here:
        bufs[chain] = take(4)
    later = [take(4) for _ in ahead]
    sems = refs[-1]
    now = {chain: loads(hbm, bufs[chain], sems.at[chain], chain, group) for chain in here}
    after = [c for n, (chain, g) in enumerate(ahead) for c in loads(hbm, later[n], sems.at[2 + n], chain, g)]
    if first:
        split_kv, split_out, bkv, bout, bsems = refs[:5]
        copies = [
            pltpu.make_async_copy(basis[0], bkv, bsems.at[0]),
            pltpu.make_async_copy(basis[1], bout, bsems.at[1]),
        ]
        for copy in copies:
            copy.start()
    for chain in here:
        for copy in now[chain]:
            copy.start()
    if not first:
        for copy in after:
            copy.start()
    if first:
        for copy in copies:
            copy.wait()
        for a in range(2):
            b = jnp.concatenate(split3(bkv[a]), axis=0)
            split_kv[a] = jnp.concatenate([b, b], axis=1)
        split_out[...] = jnp.concatenate(split3(bout[...]), axis=0)
        basis = (split_kv, split_out)

    def fold(r):
        return r[:RANK] + (r[RANK : 2 * RANK] + r[2 * RANK :])

    for chain in [*given, *here]:
        for copy in now.get(chain, []):
            copy.wait()
        if first and chain == here[0]:
            for copy in after:
                copy.start()
        gkv, ekv, gout, eout = bufs[chain]
        _, name = group_of(chain, *group)
        for j in range(GROUP):
            rows, orows = slice(j * CH, (j + 1) * CH), slice(j * OCH, (j + 1) * OCH)
            i = jnp.bitwise_xor(name, j)
            both = jnp.concatenate([gkv[rows], ekv[rows]], axis=1)
            outs[chain][i, :, :CH] = fold(dot_nt(basis[0][chain], both))
            outs[chain][i, :, CH:] = fold(dot_nt(basis[1][...], gout[orows]) + dot_nt(basis[1][...], eout[orows]))
    for copy in after:
        copy.wait()


def part(group, args, basis, bufs, ahead=(), after=(), first=False):
    given = [chain for chain in range(2) if (chain, group) in bufs]
    loaded = [(chain, group) for chain in range(2) if chain not in given] + list(ahead)
    shapes = [jax.ShapeDtypeStruct((GROUP, RANK, WIDE), F32)] * 2 + ROW_SHAPES * len(loaded)
    scratch = [pltpu.SemaphoreType.DMA((2 + len(ahead), 4))]
    if first:
        shapes.append(jax.ShapeDtypeStruct((2, 3 * RANK, 2 * COLS), BF16))
        shapes.append(jax.ShapeDtypeStruct((3 * RANK, OCOLS), BF16))
        scratch = [pltpu.VMEM((2, RANK, COLS), F32), pltpu.VMEM((RANK, OCOLS), F32), pltpu.SemaphoreType.DMA((2,))] + scratch
    operands = [x for chain in given for x in bufs[chain, group]]
    result = pl.pallas_call(
        functools.partial(part_kernel, group, given, ahead, len(after), first),
        out_shape=shapes,
        in_specs=[HBM] * 4 + [HBM if first else VM] * 2 + [VM] * (len(operands) + len(after)),
        out_specs=[VM] * len(shapes),
        scratch_shapes=scratch,
        compiler_params=pltpu.CompilerParams(vmem_limit_bytes=16 * MIB),
        cost_estimate=cost(3),
        name="part",
    )(*args, *basis, *operands, *after)
    for n, key in enumerate(loaded):
        bufs[key] = tuple(result[2 + 4 * n : 6 + 4 * n])
    return result[:2], result[2 + 4 * len(loaded) :]


def tree(items):
    while len(items) > 1:
        items = [a + b for a, b in zip(items[::2], items[1::2])]
    return items[0]


def right_kernel(chain, group, n_before, last, *refs):
    bufs, x = refs[:4], refs[4]
    before = refs[5 : 5 + n_before]
    keys = refs[5 + n_before] if last else None
    right, gram = refs[-2:]

    def fold(r):
        return r[:RANK] + r[RANK:]

    def square(parts):
        g = dot_nt(jnp.concatenate(parts, axis=0), jnp.concatenate(parts, axis=0))

        def at(i, j):
            return g[i * RANK : (i + 1) * RANK, j * RANK : (j + 1) * RANK]

        return at(0, 0) + ((at(0, 1) + at(1, 0)) + ((at(0, 2) + at(2, 0)) + at(1, 1)))

    sums = [0.0, 0.0]
    grams = [[], []]
    _, name = group_of(chain, *group)
    for j in range(GROUP):
        parts = split3(x[jnp.bitwise_xor(name, j)])
        rows, orows = slice(j * CH, (j + 1) * CH), slice(j * OCH, (j + 1) * OCH)
        kv, o = [p[:, :CH] for p in parts], [p[:, CH:] for p in parts]
        grams[0].append(square(kv))
        grams[1].append(square(o))
        both = jnp.concatenate([bufs[0][rows], bufs[1][rows]], axis=1)
        r = fold(dot(jnp.concatenate(kv[:2], axis=0), both))
        sums[0] += r[:, :COLS] + r[:, COLS:]
        two = jnp.concatenate(o[:2], axis=0)
        sums[1] += fold(dot(two, bufs[2][orows]) + dot(two, bufs[3][orows]))
    for k in range(2):
        gram[k] = tree(grams[k])
    sums = jnp.concatenate(sums, axis=1)
    for other in before:
        sums += other[...]
    if last:
        right[:, :COLS] = keys[:, :COLS]
        right[:, COLS : 2 * COLS] = sums[:, :COLS]
        right[:, 2 * COLS :] = keys[:, COLS:] + sums[:, COLS:]
    else:
        right[...] = sums


def right_part(chain, group, bufs, lead, before=(), keys=None, after=()):
    last = keys is not None
    width = 2 * COLS + OCOLS if last else COLS + OCOLS
    operands = (*bufs[chain, group], lead, *before, *([keys] if last else []), *after)
    return pl.pallas_call(
        functools.partial(right_kernel, chain, group, len(before), last),
        out_shape=(
            jax.ShapeDtypeStruct((RANK, width), F32),
            jax.ShapeDtypeStruct((2, RANK, RANK), F32),
        ),
        in_specs=[VM] * len(operands),
        out_specs=(VM, VM),
        compiler_params=pltpu.CompilerParams(vmem_limit_bytes=16 * MIB),
        cost_estimate=cost(1),
        name="right",
    )(*operands)


def factor_kernel(a0, a1, a2, a3, b0, b1, b2, b3, out):
    row = lax.broadcasted_iota(jnp.int32, (RANK, 2 * RANK), 0)
    col = lax.broadcasted_iota(jnp.int32, (RANK, 2 * RANK), 1)
    eye = jnp.where(col == row + RANK, 1.0, 0.0).astype(F32)
    keys, outs_a = [(a0[k] + a1[k]) + (a2[k] + a3[k]) for k in range(2)]
    values, outs_b = [(b0[k] + b1[k]) + (b2[k] + b3[k]) for k in range(2)]
    gram = [keys, values, outs_a + outs_b]
    wide = [jnp.concatenate([gram[k], jnp.zeros((RANK, RANK), F32)], axis=1) + eye for k in range(3)]
    scale = [jnp.zeros((RANK, 1), F32)] * 3
    below = lax.broadcasted_iota(jnp.int32, (RANK, 1), 0)
    for i in range(RANK):
        for k in range(3):
            pivot = wide[k][i : i + 1, :]
            d = wide[k][i : i + 1, i : i + 1]
            scale[k] = jnp.where(below == i, lax.rsqrt(d), scale[k])
            factor = jnp.where(below > i, wide[k][:, i : i + 1] / d, 0.0)
            wide[k] = wide[k] - factor * pivot
    for k in range(3):
        out[k] = wide[k][:, RANK:] * scale[k]


def factor(grams):
    return pl.pallas_call(
        factor_kernel,
        out_shape=jax.ShapeDtypeStruct((3, RANK, RANK), F32),
        in_specs=[VM] * 8,
        out_specs=VM,
        compiler_params=pltpu.CompilerParams(vmem_limit_bytes=4 * MIB),
        cost_estimate=cost(4),
        name="factor",
    )(*grams)


def left_kernel(dh, *refs):
    a_own, a_got, b_own, b_got, w = refs[:5]
    left_kv, left_out, ortho, bkv, bout, sems = refs[-6:]
    weights = []
    for k in range(3):
        w1, w2, w3 = split3(w[k])
        weights.append(jnp.concatenate([w1, w1, w2, w1, w2, w3], axis=1))

    def apply(k, x):
        l1, l2, l3 = split3(x)
        return dot(weights[k], jnp.concatenate([l1, l2, l1, l3, l2, l1], axis=0))

    def packed(o):
        high = o.astype(BF16).astype(F32)
        rest = o - high
        return jnp.transpose(jnp.concatenate([high, rest, high, jnp.zeros_like(o)], axis=0)).astype(BF16)

    copies = []
    for d1 in range(2):
        for s, lead in enumerate(((a_own, a_got)[d1], (b_own, b_got)[d1])):
            first, name = group_of(s, dh, d1)
            for j in range(GROUP):
                x = lead[jnp.bitwise_xor(name, j)]
                o_kv = apply(s, x[:, :CH])
                o_out = apply(2, x[:, CH:])
                bkv[d1, s, :, j * CH : (j + 1) * CH] = o_kv * (ROWS**0.5)
                bout[d1, s, :, j * OCH : (j + 1) * OCH] = o_out * (OROWS**0.5)
                ortho[d1, s, j, :CH] = packed(o_kv)
                ortho[d1, s, j, CH:] = packed(o_out)
            rows, orows = group_rows(s, first)
            copies.append(pltpu.make_async_copy(bkv.at[d1, s], left_kv.at[s, :, rows], sems.at[d1, s, 0]))
            copies.append(pltpu.make_async_copy(bout.at[d1, s], left_out.at[:, orows], sems.at[d1, s, 1]))
            copies[-2].start()
            copies[-1].start()
    for copy in copies:
        copy.wait()


def left_part(dh, lead, w, before=()):
    return pl.pallas_call(
        functools.partial(left_kernel, dh),
        out_shape=(
            jax.ShapeDtypeStruct((2, RANK, ROWS), F32),
            jax.ShapeDtypeStruct((RANK, OROWS), F32),
            jax.ShapeDtypeStruct((2, 2, GROUP, WIDE, 128), BF16),
        ),
        in_specs=[VM] * 5 + [HBM] * len(before),
        out_specs=(HBM, HBM, VM),
        scratch_shapes=[
            pltpu.VMEM((2, 2, RANK, GROUP * CH), F32),
            pltpu.VMEM((2, 2, RANK, GROUP * OCH), F32),
            pltpu.SemaphoreType.DMA((2, 2, 2)),
        ],
        input_output_aliases={5: 0, 6: 1} if before else {},
        compiler_params=pltpu.CompilerParams(vmem_limit_bytes=16 * MIB),
        cost_estimate=cost(2),
        name="left",
    )(*lead, w, *before)


def error_kernel(*refs):
    total, w, ortho = refs[32], refs[33], refs[34:36]
    right_kv, right_out, new_kv, new_out, nkv, nout, nsems = refs[36:]
    packed = []
    for k, (at, n) in enumerate(((0, COLS), (COLS, COLS), (2 * COLS, OCOLS))):
        w1, w2, w3 = split3(w[k])
        r1, r2, r3 = split3(total[:, at : at + n] * (1.0 / REPLICAS))
        right = dot(
            jnp.concatenate([w1, w1, w2, w1, w2, w3], axis=1),
            jnp.concatenate([r1, r2, r1, r3, r2, r1], axis=0),
        )
        if k < 2:
            right_kv[k] = right
        else:
            right_out[...] = right
        high, low = split2(right)
        packed.append(jnp.concatenate([high, high, low, jnp.zeros_like(high)], axis=0))
    stores = []
    for g, (dh, d1) in enumerate(GROUPS):
        for s in range(2):
            gkv, ekv, gout, eout = refs[8 * g + 4 * s : 8 * g + 4 * s + 4]
            for j in range(GROUP):
                at, oat = slice(j * CH, (j + 1) * CH), slice(j * OCH, (j + 1) * OCH)
                merged = gkv[at].astype(F32) + ekv[at].astype(F32)
                nkv[g, s, at] = (merged - dot(ortho[dh][d1, s, j, :CH], packed[s])).astype(BF16)
                merged = gout[oat].astype(F32) + eout[oat].astype(F32)
                nout[g, s, oat] = (merged - dot(ortho[dh][d1, s, j, CH:], packed[2])).astype(BF16)
            rows, orows = group_rows(s, group_of(s, dh, d1)[0])
            stores.append(pltpu.make_async_copy(nkv.at[g, s], new_kv.at[0, s, rows, :], nsems.at[g, s, 0]))
            stores.append(pltpu.make_async_copy(nout.at[g, s], new_out.at[0, orows, :], nsems.at[g, s, 1]))
            stores[-2].start()
            stores[-1].start()
    for copy in stores:
        copy.wait()


GROUPS = ((0, 0), (0, 1), (1, 0), (1, 1))


def errors(bufs, total, w, ortho):
    bufs = [x for group in GROUPS for chain in range(2) for x in bufs[chain, group]]
    return pl.pallas_call(
        error_kernel,
        out_shape=(
            jax.ShapeDtypeStruct((2, RANK, COLS), F32),
            jax.ShapeDtypeStruct((RANK, OCOLS), F32),
            jax.ShapeDtypeStruct((1, 2, ROWS, COLS), BF16),
            jax.ShapeDtypeStruct((1, OROWS, OCOLS), BF16),
        ),
        in_specs=[VM] * 36,
        out_specs=(VM, VM, HBM, HBM),
        scratch_shapes=[
            pltpu.VMEM((4, 2, GROUP * CH, COLS), BF16),
            pltpu.VMEM((4, 2, GROUP * OCH, OCOLS), BF16),
            pltpu.SemaphoreType.DMA((4, 2, 2)),
        ],
        compiler_params=pltpu.CompilerParams(vmem_limit_bytes=24 * MIB),
        cost_estimate=cost(5),
        name="errors",
    )(*bufs, total, w, *ortho)


def on_device(grad_kv, error_kv, grad_out, error_out, basis_kv, basis_out):
    args = (grad_kv, error_kv, grad_out, error_out, jnp.swapaxes(basis_kv, 1, 2), basis_out.T)
    *args, bkv, bout = [pltpu.with_memory_space_constraint(x, pltpu.HBM) for x in args]
    near0, near1, far0, far1 = GROUPS
    bufs = {}
    far, basis = part(far1, args, (bkv, bout), bufs, [(0, near1)], first=True)
    far = [send(x, CORES) for x in far]
    near, _ = part(near1, args, basis, bufs, [(0, far0)])
    sent = [x + y for x, y in zip(near, far)]
    got = [send(x, pairs(CHAINS[s], 0)) for s, x in enumerate(sent)]
    far, _ = part(far0, args, basis, bufs, [(0, near0), (1, near0)], after=sent)
    far = [send(x, CORES) for x in far]
    near, _ = part(near0, args, basis, bufs, after=got[1:])
    both = [(x + y) + z for x, y, z in zip(near, far, got)]

    for k in range(1, 2 * STEPS):
        for s in range(2):
            x = both[s]
            if k < STEPS:
                n = x.shape[0] // 2
                both[s] = x[:n] + send(x[n:], pairs(CHAINS[s], k))
            else:
                both[s] = x + send(x, pairs(CHAINS[s], k))
    for k in reversed(range(1, STEPS)):
        both = [jnp.concatenate([x, send(x, pairs(CHAINS[s], k))]) for s, x in enumerate(both)]
    own0 = both
    own1 = [send(x, pairs(CHAINS[s], 0)) for s, x in enumerate(both)]
    other0 = [send(x, CORES) for x in own0]
    other1, grams, total = [], [], None
    for s in range(2):
        sum1, gram1 = right_part(s, near0, bufs, own0[s])
        sum2, gram2 = right_part(s, far0, bufs, other0[s])
        if s == 0:
            own1[s], sum1, sum2 = lax.optimization_barrier((own1[s], sum1, sum2))
        else:
            own1[s], sum1, sum2, sum3 = lax.optimization_barrier((own1[s], sum1, sum2, sum3))
        other1.append(send(own1[s], CORES))
        sum3, gram3 = right_part(s, near1, bufs, own1[s], after=() if s == 0 else (total,))
        total, gram4 = right_part(s, far1, bufs, other1[s], (sum1, sum2, sum3), total)
        grams += [gram1, gram3, gram2, gram4]
    own = (own0[0], own1[0], own0[1], own1[1])
    other = (other0[0], other1[0], other0[1], other1[1])
    w = factor(grams)
    total = total + send(total, pairs(RIGHT, 0))
    total, w = lax.optimization_barrier((total, w))
    *left, ortho_own = left_part(0, own, w)
    total = total + send(total, pairs(RIGHT, 1))
    total, left = lax.optimization_barrier((total, left))
    left_kv, left_out, ortho_other = left_part(1, other, w, left)
    total = total + send(total, pairs(RIGHT, 2))
    total, ortho_other = lax.optimization_barrier((total, ortho_other))
    total = total + send(total, pairs(RIGHT, 3))
    right_kv, right_out, new_kv, new_out = errors(bufs, total, w, (ortho_own, ortho_other))
    return (
        jnp.swapaxes(left_kv, 1, 2),
        left_out.T,
        jnp.swapaxes(right_kv, 1, 2),
        right_out.T,
        new_kv,
        new_out,
    )


def solution(mesh):
    placed = (
        P("dp", None, None, "mp"),
        P("dp", None, None, "mp"),
        P("dp", None, "mp"),
        P("dp", None, "mp"),
        P(None, "mp", None),
        P("mp", None),
    )
    return jax.shard_map(
        on_device,
        mesh=mesh,
        in_specs=placed,
        out_specs=(
            P(),
            P(),
            P(None, "mp", None),
            P("mp", None),
            P("dp", None, None, "mp"),
            P("dp", None, "mp"),
        ),
        check_vma=False,
    )
```
